32 devices in a mesh: seq: 16 (over z, y, core), head: 2 (over x).
Axes of the slice: x: 2, y: 2, z: 4, core: 2. Of those that a mesh axis runs over, the one named last changes fastest.
Arguments:
- queries: bfloat16 [4096, 8, 4, 128], P(('seq', 'head')), may hold values from -210 to 210
- keys: bfloat16 [4096, 8, 128], P(('seq', 'head')), may hold values from -6 to 6
- values: bfloat16 [4096, 8, 128], P(('seq', 'head')), may hold values from -6 to 6
- d_attended: bfloat16 [4096, 8, 4, 128], P(('seq', 'head')), may hold values from -12 to 12
- shift_amounts: int32 [8], replicated, may hold values from 0 to 1024, as said below
Outputs:
- attended: bfloat16 [4096, 8, 4, 128], P(('seq', 'head'))
- d_queries: bfloat16 [4096, 8, 4, 128], P(('seq', 'head'))
- d_keys: bfloat16 [4096, 8, 128], P(('seq', 'head'))
- d_values: bfloat16 [4096, 8, 128], P(('seq', 'head'))
The draws below stay inside these ranges and needn't reach their ends.
Inputs may be any that keep to these rules, and one draw needn't show every extreme that they name: `shift_amounts`: each head's shift is 0 or 1024, and exactly half of the 8 heads have 2048 // 2.
All inputs are finite; a program needn't handle non-finite values.
Results may differ from the reference program's by a relative error of at most 0.034.
Values may be sent and summed in bfloat16 or wider, within the bound.
A program may use at most 128 MiB of HBM per device.

```python
import math
import jax
import jax.numpy as jnp
from jax import lax

HD = 128
KV_HEADS = 8
QPK = 4
GROUP = 2048
TOKENS = 4096


def base_keys(key):
    return jax.random.truncated_normal(key, -6.0, 6.0, (TOKENS, KV_HEADS, HD), jnp.float32)


def draw_keys(key, part):
    shared = base_keys(key)
    return shared.astype(jnp.bfloat16)


def draw_queries(key, part):
    key = jax.random.fold_in(key, 5)
    drawn = jax.random.truncated_normal(key, -6.0, 6.0, (TOKENS, KV_HEADS, QPK, HD), jnp.float32)
    return drawn.astype(jnp.bfloat16)


def draw_shift_amounts(key, part):
    key = jax.random.fold_in(key, 7)
    order = jax.random.permutation(key, KV_HEADS)
    return jnp.where(order < KV_HEADS // 2, GROUP // 2, 0).astype(jnp.int32)


def steps_of(stream_key, shape, cuts, low, high):
    def one(axis_at, shards_of):
        draws = jax.random.uniform(jax.random.fold_in(jax.random.fold_in(stream_key, 6), axis_at), (shards_of,), jnp.float32, low / len(cuts), high / len(cuts))
        return jnp.repeat(jnp.exp(draws), shape[axis_at] // shards_of).reshape((-1,) + (1,) * (len(shape) - axis_at - 1))

    loudness = one(*cuts[0])
    for cut in cuts[1:]:
        loudness = loudness * one(*cut)
    return loudness


def normal_values(rng, extent, width, reach, cuts=(), held_as=jnp.bfloat16):
    entries = jax.random.normal(rng, extent, jnp.float32) * width
    if len(cuts) > 0:
        entries = steps_of(rng, extent, cuts, -0.22, 0.18) * entries
    return jnp.clip(entries, min=-reach, max=reach).astype(held_as)


def setup_inputs(seed: int = 0) -> dict:
    streams_of = jax.random.split(jax.random.key(seed), 6)
    queries = draw_queries(jax.random.fold_in(streams_of[5], 71), 0)
    keys = draw_keys(jax.random.fold_in(streams_of[5], 71), 0)
    values = normal_values(streams_of[2], (TOKENS, KV_HEADS, HD), 1.0, 6.0, ((0, 32),))
    d_attended = normal_values(streams_of[3], (TOKENS, KV_HEADS, QPK, HD), 2.0, 12.0, ((0, 32),))
    shift_amounts = draw_shift_amounts(jax.random.fold_in(streams_of[5], 71), 0)
    return dict(queries=queries, keys=keys, values=values, d_attended=d_attended, shift_amounts=shift_amounts)


MASKED_LOGIT = -1e+30

def group_pass(block):
    q_block, k_block, v_block, d_block = block
    scaling = 1.0 / math.sqrt(HD)
    q_float = q_block.astype(jnp.float32)
    k_float = k_block.astype(jnp.float32)
    v_float = v_block.astype(jnp.float32)
    d_float = d_block.astype(jnp.float32)
    logits = jnp.einsum('tgd,ud->gtu', q_float, k_float) * scaling
    places = jnp.arange(GROUP, dtype=jnp.int32)
    causal = places[None, :] <= places[:, None]
    logits = jnp.where(causal[None], logits, MASKED_LOGIT)
    highest = lax.optimization_barrier(jnp.max(logits, axis=2, keepdims=True))
    lse = highest + jnp.log(lax.optimization_barrier(jnp.sum(jnp.exp(logits - highest), axis=2, keepdims=True)))
    exact_probs = jnp.exp(logits - lse)
    prob_rounded = lax.optimization_barrier(exact_probs.astype(jnp.bfloat16)).astype(jnp.float32)
    attended = jnp.einsum('gtu,ud->tgd', prob_rounded, v_float).astype(jnp.bfloat16)
    row_dot = lax.optimization_barrier(jnp.sum(d_float * attended.astype(jnp.float32), axis=2))
    d_probs = jnp.einsum('tgd,ud->gtu', d_float, v_float)
    d_scores = exact_probs * (d_probs - jnp.transpose(row_dot)[:, :, None])
    d_scores = lax.optimization_barrier(d_scores.astype(jnp.bfloat16)).astype(jnp.float32)
    d_queries = (jnp.einsum('gtu,ud->tgd', d_scores, k_float) * scaling).astype(jnp.bfloat16)
    d_keys = (jnp.einsum('gtu,tgd->ud', d_scores, q_float) * scaling).astype(jnp.bfloat16)
    d_values = jnp.einsum('gtu,tgd->ud', prob_rounded, d_float).astype(jnp.bfloat16)
    return (attended, d_queries, d_keys, d_values)

def head_pass(inputs):
    q_head, k_head, v_head, d_head, shift_value = inputs
    groups = TOKENS // GROUP
    rolled = [jnp.roll(item, -shift_value, axis=0) for item in (q_head, k_head, v_head, d_head)]
    shaped = [item.reshape((groups, GROUP) + item.shape[1:]) for item in rolled]
    results = lax.map(group_pass, tuple(shaped))
    return tuple((jnp.roll(item.reshape((TOKENS,) + item.shape[2:]), shift_value, axis=0) for item in results))

def reference(queries, keys, values, d_attended, shift_amounts):
    by_head = (jnp.moveaxis(queries, 1, 0), jnp.moveaxis(keys, 1, 0), jnp.moveaxis(values, 1, 0), jnp.moveaxis(d_attended, 1, 0), shift_amounts.astype(jnp.int32))
    attended, d_queries, d_keys, d_values = lax.map(head_pass, by_head)
    return (jnp.moveaxis(attended, 0, 1), jnp.moveaxis(d_queries, 0, 1), jnp.moveaxis(d_keys, 0, 1), jnp.moveaxis(d_values, 0, 1))
```

```python
import functools
import math

import jax
import jax.numpy as jnp
from jax import lax
from jax.experimental import pallas as pl
from jax.experimental.pallas import tpu as pltpu
from jax.sharding import PartitionSpec as P

GROUP = 2048
HALF = GROUP // 2
CHUNK = 256
MASKED = -1e30
MESH = pl.DeviceIdType.MESH


def nt(a, b):
    return lax.dot_general(a, b, (((1,), (0,)), ((), ())), preferred_element_type=jnp.float32)


def tn(a, b):
    return lax.dot_general(a, b, (((0,), (0,)), ((), ())), preferred_element_type=jnp.float32)


def kernel(
    n_seq, n_head, tok,
    shift_ref, q_ref, k_ref, v_ref, d_ref,
    o_ref, dq_ref, dk_ref, dv_ref,
    kv, part, sib, red, rb_own, rb_far, scores, o_tr, dq_tr, o_buf, dq_buf, fin, perm, inv,
    own_s, own_r, far_s, far_r, fwd_s, fwd_r, ffwd_s, ffwd_r,
    sib_s, sib_r, fsib_s, fsib_r, back_s, back_r, fback_s, fback_r,
):
    heads = k_ref.shape[0]
    near = heads // 2
    nq = q_ref.shape[1]
    span = HALF // (tok * n_head)
    rows = tok * n_head
    pairs = span // 2
    chips = pairs * n_head
    n_planes = n_seq // span
    seq = lax.axis_index("seq")
    x = lax.axis_index("head")
    plane = seq // span
    s_in = seq % span
    y = s_in // 2
    core = s_in % 2
    chip = y * n_head + x
    pos = s_in * n_head + x
    nxt = (plane + 1) % n_planes
    prv = (plane + n_planes - 1) % n_planes
    scaling = 1.0 / math.sqrt(k_ref.shape[2])
    to_exp2 = scaling * math.log2(math.e)

    def device(at_plane, at_chip):
        return (at_plane * span + (at_chip // n_head) * 2 + core, at_chip % n_head)

    sibling = (plane * span + y * 2 + 1 - core, x)

    def place(at_chip):
        return ((at_chip // n_head) * 2 + core) * n_head + at_chip % n_head

    barrier = pltpu.get_barrier_semaphore()
    pl.semaphore_signal(barrier, inc=1, device_id=sibling, device_id_type=MESH)
    for k in range(chips):
        other = (chip + k) % chips
        if k:
            pl.semaphore_signal(barrier, inc=1, device_id=device(plane, other), device_id_type=MESH)
        pl.semaphore_signal(barrier, inc=1, device_id=device(nxt, other), device_id_type=MESH)
        pl.semaphore_signal(barrier, inc=1, device_id=device(prv, other), device_id_type=MESH)

    even = plane % 2 == 0
    n_near = jnp.int32(0)
    n_far = jnp.int32(0)
    ranks = []
    for h in range(heads):
        is_near = (shift_ref[h] == 0) == even
        ranks.append(jnp.where(is_near, n_near, (near + n_far) % heads))
        n_near = n_near + is_near.astype(jnp.int32)
        n_far = n_far + 1 - is_near.astype(jnp.int32)
    for h in range(heads):
        inv[h] = ranks[h]
        perm[h] = sum(jnp.where(ranks[j] == h, j, 0) for j in range(heads))

    mine = pl.ds(pl.multiple_of(HALF + pos * tok, tok), tok)
    for i in range(heads):
        kv[i, 0, mine, :] = k_ref[perm[i]]
        kv[i, 1, mine, :] = v_ref[perm[i]]

    def remote(src, dst, ssem, rsem, dev):
        return pltpu.make_async_remote_copy(
            src_ref=src, dst_ref=dst, send_sem=ssem, recv_sem=rsem, device_id=dev, device_id_type=MESH
        )

    def own_copy(i, to):
        view = kv.at[i, :, mine, :]
        return remote(view, view, own_s.at[i, to], own_r.at[i, chip], device(plane, to))

    def own_arrival(i, source):
        view = kv.at[i, :, pl.ds(pl.multiple_of(HALF + place(source) * tok, tok), tok), :]
        return remote(view, view, own_s.at[i, source], own_r.at[i, source], device(plane, source))

    def far_copy(i, to):
        return remote(
            kv.at[i, :, mine, :],
            kv.at[i + near, :, pl.ds(pl.multiple_of(pos * tok, tok), tok), :],
            far_s.at[i, to], far_r.at[i, chip], device(nxt, to),
        )

    def far_arrival(i, source):
        view = kv.at[i, :, pl.ds(pl.multiple_of(place(source) * tok, tok), tok), :]
        return remote(view, view, far_s.at[i - near, source], far_r.at[i - near, source], device(prv, source))

    def strip(base, at_pair, parity):
        return pl.ds(pl.multiple_of(base + (at_pair * 2 + parity) * rows, rows), rows)

    def forward(i, at_pair, parity):
        view = kv.at[i, :, strip(HALF, at_pair, parity), :]
        return remote(view, view, fwd_s.at[i, at_pair], fwd_r.at[i, at_pair], sibling)

    def far_forward(i, at_pair, parity):
        view = kv.at[i, :, strip(0, at_pair, parity), :]
        return remote(view, view, ffwd_s.at[i - near, at_pair], ffwd_r.at[i - near, at_pair], sibling)

    def packed(region, at_pair):
        return pl.ds((region * pairs + at_pair) * rows, rows)

    def sib_copy(i, at_pair):
        return remote(
            part.at[i, :, strip(HALF, at_pair, 1 - core), :], sib.at[i, :, packed(1, at_pair), :],
            sib_s.at[i, at_pair], sib_r.at[i, at_pair], sibling,
        )

    def far_sib_copy(i, at_pair):
        return remote(
            part.at[i, :, strip(0, at_pair, 1 - core), :], sib.at[i, :, packed(0, at_pair), :],
            fsib_s.at[i - near, at_pair], fsib_r.at[i - near, at_pair], sibling,
        )

    def red_rows(region, at_chip):
        return pl.ds(pl.multiple_of(region * (HALF // 2) + at_chip * tok, tok), tok)

    def back_copy(i, to):
        return remote(
            red.at[i, :, red_rows(1, to), :], rb_own.at[i, chip],
            back_s.at[i, to], back_r.at[i, chip], device(plane, to),
        )

    def back_arrival(i, source):
        return remote(
            red.at[i, :, red_rows(1, source), :], rb_own.at[i, source],
            back_s.at[i, source], back_r.at[i, source], device(plane, source),
        )

    def far_back_copy(i, to):
        return remote(
            red.at[i, :, red_rows(0, to), :], rb_far.at[i - near, chip],
            fback_s.at[i - near, to], fback_r.at[i - near, chip], device(prv, to),
        )

    def far_back_arrival(i, source):
        return remote(
            red.at[i, :, red_rows(0, source), :], rb_far.at[i, source],
            fback_s.at[i, source], fback_r.at[i, source], device(nxt, source),
        )

    pl.semaphore_wait(barrier, 3 * chips)

    @pl.loop(0, heads)
    def _(i):
        for k in range(1, chips):
            own_copy(i, (chip + k) % chips).start()

    @pl.loop(0, near)
    def _(i):
        for k in range(chips):
            far_copy(i, (chip + k) % chips).start()

    def start_forwards(i):
        for k in range(1, chips):
            own_arrival(i, (chip + k) % chips).wait_recv()
        for at_pair in range(pairs):
            forward(i, at_pair, core).start()

        @pl.when(i >= near)
        def _():
            for k in range(chips):
                far_arrival(i, (chip + k) % chips).wait_recv()
            for at_pair in range(pairs):
                far_forward(i, at_pair, core).start()

    def pass_on(i):
        for at_pair in range(pairs):
            sib_copy(i, at_pair).wait_recv()
            for w in range(2):
                red[i, w, packed(1, at_pair), :] = (
                    part[i, w, strip(HALF, at_pair, core), :].astype(jnp.float32)
                    + sib[i, w, packed(1, at_pair), :].astype(jnp.float32)
                ).astype(jnp.bfloat16)
        for k in range(1, chips):
            back_copy(i, (chip + k) % chips).start()

        @pl.when(i >= near)
        def _():
            for at_pair in range(pairs):
                far_sib_copy(i, at_pair).wait_recv()
                for w in range(2):
                    red[i, w, packed(0, at_pair), :] = (
                        part[i, w, strip(0, at_pair, core), :].astype(jnp.float32)
                        + sib[i, w, packed(0, at_pair), :].astype(jnp.float32)
                    ).astype(jnp.bfloat16)
            for k in range(chips):
                far_back_copy(i, (chip + k) % chips).start()

    start_forwards(0)
    ahead = lax.broadcasted_iota(jnp.int32, (CHUNK, nq), 0) - HALF - pos * tok
    ahead = ahead - lax.broadcasted_iota(jnp.int32, (CHUNK, nq), 1) % tok
    n_chunks = GROUP // CHUNK

    @pl.loop(0, heads)
    def _(i):
        head = perm[i]
        q = q_ref[head]
        d = d_ref[head]
        q_tr = q.T
        d_tr = d.T
        first = jnp.where(i < near, HALF // CHUNK, 0)
        for at_pair in range(pairs):
            forward(i, at_pair, 1 - core).wait_recv()

        @pl.when(i >= near)
        def _():
            for at_pair in range(pairs):
                far_forward(i, at_pair, 1 - core).wait_recv()

        def score_step(c, top):
            at = pl.ds(pl.multiple_of(c * CHUNK, CHUNK), CHUNK)
            s = nt(kv[i, 0, at, :], q_tr)
            s = jnp.where(ahead <= -c * CHUNK, s, MASKED)
            scores[at, :] = s
            return jnp.maximum(top, jnp.max(s.reshape(CHUNK // 8, 8, nq), axis=0))

        top = lax.fori_loop(first, n_chunks, score_step, jnp.full((8, nq), MASKED, jnp.float32))
        top = jnp.max(top, axis=0, keepdims=True)
        o_tr[...] = jnp.zeros_like(o_tr)

        def prob_step(c, total):
            at = pl.ds(pl.multiple_of(c * CHUNK, CHUNK), CHUNK)
            p = jnp.exp2((scores[at, :] - top) * to_exp2)
            scores[at, :] = p
            o_tr[...] += tn(kv[i, 1, at, :], p.astype(jnp.bfloat16))
            return total + jnp.sum(p.reshape(CHUNK // 8, 8, nq), axis=0)

        total = lax.fori_loop(first, n_chunks, prob_step, jnp.zeros((8, nq), jnp.float32))
        inverse = 1.0 / jnp.sum(total, axis=0, keepdims=True)
        attended = (o_tr[...] * inverse).astype(jnp.bfloat16)
        o_buf[i] = attended.T
        row_dot = jnp.sum(attended.astype(jnp.float32) * d_tr.astype(jnp.float32), axis=0, keepdims=True)
        dq_tr[...] = jnp.zeros_like(dq_tr)

        @pl.when(i < heads - 1)
        def _():
            start_forwards(i + 1)

        @pl.loop(first, n_chunks)
        def _(c):
            at = pl.ds(pl.multiple_of(c * CHUNK, CHUNK), CHUNK)
            k_part = kv[i, 0, at, :]
            p = scores[at, :] * inverse
            ds = (p * (nt(kv[i, 1, at, :], d_tr) - row_dot)).astype(jnp.bfloat16)
            part[i, 1, at, :] = nt(p.astype(jnp.bfloat16), d).astype(jnp.bfloat16)
            part[i, 0, at, :] = (nt(ds, q) * scaling).astype(jnp.bfloat16)
            dq_tr[...] += tn(k_part, ds)

        dq_buf[i] = (dq_tr[...] * scaling).astype(jnp.bfloat16).T
        for at_pair in range(pairs):
            sib_copy(i, at_pair).start()

        @pl.when(i >= near)
        def _():
            for at_pair in range(pairs):
                far_sib_copy(i, at_pair).start()

        @pl.when(i > 0)
        def _():
            pass_on(i - 1)

    pass_on(heads - 1)
    for h in range(heads):
        o_ref[h] = o_buf[inv[h]]
        dq_ref[h] = dq_buf[inv[h]]

    @pl.loop(0, heads)
    def _(i):
        for w in range(2):
            fin[i, w] = red[i, w, red_rows(1, chip), :].astype(jnp.float32)
        for k in range(1, chips):
            source = (chip + k) % chips
            back_arrival(i, source).wait_recv()
            for w in range(2):
                fin[i, w] += rb_own[i, source, w].astype(jnp.float32)

        @pl.when(i < near)
        def _():
            for k in range(chips):
                source = (chip + k) % chips
                far_back_arrival(i, source).wait_recv()
                for w in range(2):
                    fin[i, w] += rb_far[i, source, w].astype(jnp.float32)

    for h in range(heads):
        dk_ref[h] = fin[inv[h], 0].astype(jnp.bfloat16)
        dv_ref[h] = fin[inv[h], 1].astype(jnp.bfloat16)

    @pl.loop(0, heads)
    def _(i):
        for k in range(1, chips):
            to = (chip + k) % chips
            own_copy(i, to).wait_send()
            back_copy(i, to).wait_send()
        for at_pair in range(pairs):
            forward(i, at_pair, core).wait_send()
            sib_copy(i, at_pair).wait_send()

        @pl.when(i < near)
        def _():
            for k in range(chips):
                far_copy(i, (chip + k) % chips).wait_send()

        @pl.when(i >= near)
        def _():
            for k in range(chips):
                far_back_copy(i, (chip + k) % chips).wait_send()
            for at_pair in range(pairs):
                far_forward(i, at_pair, core).wait_send()
                far_sib_copy(i, at_pair).wait_send()


def local(n_seq, n_head, queries, keys, values, d_attended, shift_amounts):
    tok, heads, per, hd = queries.shape
    near = heads // 2
    nq = per * tok
    pairs = HALF // (tok * n_head) // 2
    chips = pairs * n_head

    def rows_first(a):
        return jnp.transpose(a, (1, 2, 0, 3)).reshape(heads, nq, hd)

    def tokens_first(a):
        return jnp.transpose(a.reshape(heads, per, tok, hd), (2, 0, 1, 3))

    vmem = pl.BlockSpec(memory_space=pltpu.VMEM)
    bf16, f32 = jnp.bfloat16, jnp.float32
    dma = pltpu.SemaphoreType.DMA
    wide = jax.ShapeDtypeStruct((heads, nq, hd), bf16)
    thin = jax.ShapeDtypeStruct((heads, tok, hd), bf16)
    o, dq, dk, dv = pl.pallas_call(
        functools.partial(kernel, n_seq, n_head, tok),
        out_shape=(wide, wide, thin, thin),
        in_specs=[pl.BlockSpec(memory_space=pltpu.SMEM)] + [vmem] * 4,
        out_specs=(vmem,) * 4,
        scratch_shapes=[
            pltpu.VMEM((heads, 2, GROUP, hd), bf16),
            pltpu.VMEM((heads, 2, GROUP, hd), bf16),
            pltpu.VMEM((heads, 2, HALF, hd), bf16),
            pltpu.VMEM((heads, 2, HALF, hd), bf16),
            pltpu.VMEM((heads, chips, 2, tok, hd), bf16),
            pltpu.VMEM((near, chips, 2, tok, hd), bf16),
            pltpu.VMEM((GROUP, nq), f32),
            pltpu.VMEM((hd, nq), f32),
            pltpu.VMEM((hd, nq), f32),
            pltpu.VMEM((heads, nq, hd), bf16),
            pltpu.VMEM((heads, nq, hd), bf16),
            pltpu.VMEM((heads, 2, tok, hd), f32),
            pltpu.SMEM((heads,), jnp.int32),
            pltpu.SMEM((heads,), jnp.int32),
            dma((heads, chips)), dma((heads, chips)), dma((near, chips)), dma((near, chips)),
            dma((heads, pairs)), dma((heads, pairs)), dma((near, pairs)), dma((near, pairs)),
            dma((heads, pairs)), dma((heads, pairs)), dma((near, pairs)), dma((near, pairs)),
            dma((heads, chips)), dma((heads, chips)), dma((near, chips)), dma((near, chips)),
        ],
        compiler_params=pltpu.CompilerParams(
            collective_id=0, has_side_effects=True, vmem_limit_bytes=56 * 1024 * 1024
        ),
    )(
        shift_amounts,
        rows_first(queries),
        jnp.transpose(keys, (1, 0, 2)),
        jnp.transpose(values, (1, 0, 2)),
        rows_first(d_attended),
    )
    return (
        tokens_first(o),
        tokens_first(dq),
        jnp.transpose(dk, (1, 0, 2)),
        jnp.transpose(dv, (1, 0, 2)),
    )


def solution(mesh):
    wide = P(("seq", "head"), None, None, None)
    thin = P(("seq", "head"), None, None)
    return jax.shard_map(
        functools.partial(local, mesh.shape["seq"], mesh.shape["head"]),
        mesh=mesh,
        in_specs=(wide, thin, thin, wide, P()),
        out_specs=(wide, wide, thin, thin),
        check_vma=False,
    )
```

```python
import functools
import math

import jax
import jax.numpy as jnp
from jax import lax
from jax.experimental import pallas as pl
from jax.experimental.pallas import tpu as pltpu
from jax.sharding import PartitionSpec as P

GROUP = 2048
HALF = GROUP // 2
CHUNK = 512
MASKED = -1e30
MESH = pl.DeviceIdType.MESH


def nt(a, b):
    return lax.dot_general(a, b, (((1,), (0,)), ((), ())), preferred_element_type=jnp.float32)


def tn(a, b):
    return lax.dot_general(a, b, (((0,), (0,)), ((), ())), preferred_element_type=jnp.float32)


def kernel(
    n_seq, n_head, tok,
    shift_ref, q_ref, k_ref, v_ref, d_ref,
    o_ref, dq_ref, dk_ref, dv_ref,
    kv, part, sib, red, rb_own, rb_far, scores, o_tr, dq_tr, o_buf, dq_buf, fin, k_by, v_by, perm, inv,
    own_s, own_r, far_s, far_r, fwd_s, fwd_r, ffwd_s, ffwd_r,
    sib_s, sib_r, fsib_s, fsib_r, back_s, back_r, fback_s, fback_r,
):
    heads = k_ref.shape[1]
    near = heads // 2
    per = q_ref.shape[2]
    nq = per * tok
    span = HALF // (tok * n_head)
    rows = tok * n_head
    pairs = span // 2
    chips = pairs * n_head
    n_planes = n_seq // span
    seq = lax.axis_index("seq")
    x = lax.axis_index("head")
    plane = seq // span
    s_in = seq % span
    y = s_in // 2
    core = s_in % 2
    chip = y * n_head + x
    pos = s_in * n_head + x
    nxt = (plane + 1) % n_planes
    prv = (plane + n_planes - 1) % n_planes
    hd = k_ref.shape[2]
    scaling = 1.0 / math.sqrt(hd)
    to_exp2 = scaling * math.log2(math.e)

    def device(at_plane, at_chip):
        return (at_plane * span + (at_chip // n_head) * 2 + core, at_chip % n_head)

    sibling = (plane * span + y * 2 + 1 - core, x)

    def place(at_chip):
        return ((at_chip // n_head) * 2 + core) * n_head + at_chip % n_head

    barrier = pltpu.get_barrier_semaphore()
    pl.semaphore_signal(barrier, inc=1, device_id=sibling, device_id_type=MESH)
    for k in range(chips):
        other = (chip + k) % chips
        if k:
            pl.semaphore_signal(barrier, inc=1, device_id=device(plane, other), device_id_type=MESH)
        pl.semaphore_signal(barrier, inc=1, device_id=device(nxt, other), device_id_type=MESH)
        pl.semaphore_signal(barrier, inc=1, device_id=device(prv, other), device_id_type=MESH)

    even = plane % 2 == 0
    n_near = jnp.int32(0)
    n_far = jnp.int32(0)
    ranks = []
    for h in range(heads):
        is_near = (shift_ref[h] == 0) == even
        ranks.append(jnp.where(is_near, n_near, (near + n_far) % heads))
        n_near = n_near + is_near.astype(jnp.int32)
        n_far = n_far + 1 - is_near.astype(jnp.int32)
    for h in range(heads):
        inv[h] = ranks[h]
        perm[h] = sum(jnp.where(ranks[j] == h, j, 0) for j in range(heads))

    k_by[...] = jnp.swapaxes(k_ref[...].astype(jnp.float32), 0, 1).astype(jnp.bfloat16)
    v_by[...] = jnp.swapaxes(v_ref[...].astype(jnp.float32), 0, 1).astype(jnp.bfloat16)
    mine = pl.ds(pl.multiple_of(HALF + pos * tok, tok), tok)
    for i in range(heads):
        kv[i, 0, mine, :] = k_by[perm[i]]
        kv[i, 1, mine, :] = v_by[perm[i]]

    def remote(src, dst, ssem, rsem, dev):
        return pltpu.make_async_remote_copy(
            src_ref=src, dst_ref=dst, send_sem=ssem, recv_sem=rsem, device_id=dev, device_id_type=MESH
        )

    def own_copy(i, to):
        view = kv.at[i, :, mine, :]
        return remote(view, view, own_s.at[i, to], own_r.at[i, chip], device(plane, to))

    def own_arrival(i, source):
        view = kv.at[i, :, pl.ds(pl.multiple_of(HALF + place(source) * tok, tok), tok), :]
        return remote(view, view, own_s.at[i, source], own_r.at[i, source], device(plane, source))

    def far_copy(i, to):
        return remote(
            kv.at[i, :, mine, :],
            kv.at[i + near, :, pl.ds(pl.multiple_of(pos * tok, tok), tok), :],
            far_s.at[i, to], far_r.at[i, chip], device(nxt, to),
        )

    def far_arrival(i, source):
        view = kv.at[i, :, pl.ds(pl.multiple_of(place(source) * tok, tok), tok), :]
        return remote(view, view, far_s.at[i - near, source], far_r.at[i - near, source], device(prv, source))

    def strip(base, at_pair, parity):
        return pl.ds(pl.multiple_of(base + (at_pair * 2 + parity) * rows, rows), rows)

    def forward(i, at_pair, parity):
        view = kv.at[i, :, strip(HALF, at_pair, parity), :]
        return remote(view, view, fwd_s.at[i, at_pair], fwd_r.at[i, at_pair], sibling)

    def far_forward(i, at_pair, parity):
        view = kv.at[i, :, strip(0, at_pair, parity), :]
        return remote(view, view, ffwd_s.at[i - near, at_pair], ffwd_r.at[i - near, at_pair], sibling)

    def packed(region, at_pair):
        return pl.ds((region * pairs + at_pair) * rows, rows)

    def sib_copy(i, at_pair):
        return remote(
            part.at[i, :, strip(HALF, at_pair, 1 - core), :], sib.at[i, :, packed(1, at_pair), :],
            sib_s.at[i, at_pair], sib_r.at[i, at_pair], sibling,
        )

    def far_sib_copy(i, at_pair):
        return remote(
            part.at[i, :, strip(0, at_pair, 1 - core), :], sib.at[i, :, packed(0, at_pair), :],
            fsib_s.at[i - near, at_pair], fsib_r.at[i - near, at_pair], sibling,
        )

    def red_rows(region, at_chip):
        return pl.ds(pl.multiple_of(region * (HALF // 2) + at_chip * tok, tok), tok)

    def back_copy(i, to):
        return remote(
            red.at[i, :, red_rows(1, to), :], rb_own.at[i, chip],
            back_s.at[i, to], back_r.at[i, chip], device(plane, to),
        )

    def back_arrival(i, source):
        return remote(
            red.at[i, :, red_rows(1, source), :], rb_own.at[i, source],
            back_s.at[i, source], back_r.at[i, source], device(plane, source),
        )

    def far_back_copy(i, to):
        return remote(
            red.at[i, :, red_rows(0, to), :], rb_far.at[i - near, chip],
            fback_s.at[i - near, to], fback_r.at[i - near, chip], device(prv, to),
        )

    def far_back_arrival(i, source):
        return remote(
            red.at[i, :, red_rows(0, source), :], rb_far.at[i, source],
            fback_s.at[i, source], fback_r.at[i, source], device(nxt, source),
        )

    pl.semaphore_wait(barrier, 3 * chips)

    @pl.loop(0, heads)
    def _(i):
        for k in range(1, chips):
            to = (chip + k) % chips

            @pl.when(to // n_head >= y)
            def _():
                own_copy(i, to).start()

    @pl.loop(0, near)
    def _(i):
        for k in range(chips):
            far_copy(i, (chip + k) % chips).start()

    def start_forwards(i):
        for k in range(1, chips):
            source = (chip + k) % chips

            @pl.when(source // n_head <= y)
            def _():
                own_arrival(i, source).wait_recv()

        for at_pair in range(pairs):

            @pl.when(at_pair <= y)
            def _():
                forward(i, at_pair, core).start()

        @pl.when(i >= near)
        def _():
            for k in range(chips):
                far_arrival(i, (chip + k) % chips).wait_recv()
            for at_pair in range(pairs):
                far_forward(i, at_pair, core).start()

    def pass_on(i):
        for at_pair in range(pairs):

            @pl.when(at_pair <= y)
            def _():
                sib_copy(i, at_pair).wait_recv()
                for w in range(2):
                    red[i, w, packed(1, at_pair), :] = (
                        part[i, w, strip(HALF, at_pair, core), :].astype(jnp.float32)
                        + sib[i, w, packed(1, at_pair), :].astype(jnp.float32)
                    ).astype(jnp.bfloat16)

        for k in range(1, chips):
            to = (chip + k) % chips

            @pl.when(to // n_head <= y)
            def _():
                back_copy(i, to).start()

        @pl.when(i >= near)
        def _():
            for at_pair in range(pairs):
                far_sib_copy(i, at_pair).wait_recv()
                for w in range(2):
                    red[i, w, packed(0, at_pair), :] = (
                        part[i, w, strip(0, at_pair, core), :].astype(jnp.float32)
                        + sib[i, w, packed(0, at_pair), :].astype(jnp.float32)
                    ).astype(jnp.bfloat16)
            for k in range(chips):
                far_back_copy(i, (chip + k) % chips).start()

    start_forwards(0)
    ahead = lax.broadcasted_iota(jnp.int32, (CHUNK, nq), 0) - HALF - pos * tok
    ahead = ahead - lax.broadcasted_iota(jnp.int32, (CHUNK, nq), 1) // per
    n_chunks = (HALF + (y + 1) * 2 * rows) // CHUNK

    @pl.loop(0, heads)
    def _(i):
        head = perm[i]
        q = q_ref[:, head].reshape(nq, hd)
        d = d_ref[:, head].reshape(nq, hd)
        q_tr = q.T
        d_tr = d.T
        first = jnp.where(i < near, HALF // CHUNK, 0)
        for at_pair in range(pairs):

            @pl.when(at_pair <= y)
            def _():
                forward(i, at_pair, 1 - core).wait_recv()

        @pl.when(i >= near)
        def _():
            for at_pair in range(pairs):
                far_forward(i, at_pair, 1 - core).wait_recv()

        def score_step(c, top):
            at = pl.ds(pl.multiple_of(c * CHUNK, CHUNK), CHUNK)
            s = nt(kv[i, 0, at, :], q_tr)
            s = jnp.where(ahead <= -c * CHUNK, s, MASKED)
            scores[at, :] = s
            return jnp.maximum(top, jnp.max(s.reshape(CHUNK // 8, 8, nq), axis=0))

        top = lax.fori_loop(first, n_chunks, score_step, jnp.full((8, nq), MASKED, jnp.float32))
        top = jnp.max(top, axis=0, keepdims=True)
        o_tr[...] = jnp.zeros_like(o_tr)

        def prob_step(c, total):
            at = pl.ds(pl.multiple_of(c * CHUNK, CHUNK), CHUNK)
            p = jnp.exp2((scores[at, :] - top) * to_exp2)
            scores[at, :] = p
            o_tr[...] += tn(kv[i, 1, at, :], p.astype(jnp.bfloat16))
            return total + jnp.sum(p.reshape(CHUNK // 8, 8, nq), axis=0)

        total = lax.fori_loop(first, n_chunks, prob_step, jnp.zeros((8, nq), jnp.float32))
        inverse = 1.0 / jnp.sum(total, axis=0, keepdims=True)
        attended = (o_tr[...] * inverse).astype(jnp.bfloat16)
        o_buf[i] = attended.T
        row_dot = jnp.sum(attended.astype(jnp.float32) * d_tr.astype(jnp.float32), axis=0, keepdims=True)
        dq_tr[...] = jnp.zeros_like(dq_tr)

        @pl.when(i < heads - 1)
        def _():
            start_forwards(i + 1)

        @pl.loop(first, n_chunks)
        def _(c):
            at = pl.ds(pl.multiple_of(c * CHUNK, CHUNK), CHUNK)
            k_part = kv[i, 0, at, :]
            p = scores[at, :] * inverse
            ds = (p * (nt(kv[i, 1, at, :], d_tr) - row_dot)).astype(jnp.bfloat16)
            part[i, 1, at, :] = nt(p.astype(jnp.bfloat16), d).astype(jnp.bfloat16)
            part[i, 0, at, :] = (nt(ds, q) * scaling).astype(jnp.bfloat16)
            dq_tr[...] += tn(k_part, ds)

        dq_buf[i] = (dq_tr[...] * scaling).astype(jnp.bfloat16).T
        for at_pair in range(pairs):

            @pl.when(at_pair <= y)
            def _():
                sib_copy(i, at_pair).start()

        @pl.when(i >= near)
        def _():
            for at_pair in range(pairs):
                far_sib_copy(i, at_pair).start()

        @pl.when(i > 0)
        def _():
            pass_on(i - 1)

    pass_on(heads - 1)
    for h in range(heads):
        o_ref[:, h] = o_buf[inv[h]].reshape(tok, per, hd)
        dq_ref[:, h] = dq_buf[inv[h]].reshape(tok, per, hd)

    @pl.loop(0, heads)
    def _(i):
        for w in range(2):
            fin[i, w] = red[i, w, red_rows(1, chip), :].astype(jnp.float32)
        for k in range(1, chips):
            source = (chip + k) % chips

            @pl.when(source // n_head >= y)
            def _():
                back_arrival(i, source).wait_recv()
                for w in range(2):
                    fin[i, w] += rb_own[i, source, w].astype(jnp.float32)

        @pl.when(i < near)
        def _():
            for k in range(chips):
                source = (chip + k) % chips
                far_back_arrival(i, source).wait_recv()
                for w in range(2):
                    fin[i, w] += rb_far[i, source, w].astype(jnp.float32)

    dk_ref[...] = jnp.swapaxes(jnp.stack([fin[inv[h], 0] for h in range(heads)]), 0, 1).astype(jnp.bfloat16)
    dv_ref[...] = jnp.swapaxes(jnp.stack([fin[inv[h], 1] for h in range(heads)]), 0, 1).astype(jnp.bfloat16)

    @pl.loop(0, heads)
    def _(i):
        for k in range(1, chips):
            to = (chip + k) % chips

            @pl.when(to // n_head >= y)
            def _():
                own_copy(i, to).wait_send()

            @pl.when(to // n_head <= y)
            def _():
                back_copy(i, to).wait_send()

        for at_pair in range(pairs):

            @pl.when(at_pair <= y)
            def _():
                forward(i, at_pair, core).wait_send()
                sib_copy(i, at_pair).wait_send()

        @pl.when(i < near)
        def _():
            for k in range(chips):
                far_copy(i, (chip + k) % chips).wait_send()

        @pl.when(i >= near)
        def _():
            for k in range(chips):
                far_back_copy(i, (chip + k) % chips).wait_send()
            for at_pair in range(pairs):
                far_forward(i, at_pair, core).wait_send()
                far_sib_copy(i, at_pair).wait_send()


def local(n_seq, n_head, queries, keys, values, d_attended, shift_amounts):
    tok, heads, per, hd = queries.shape
    near = heads // 2
    nq = per * tok
    pairs = HALF // (tok * n_head) // 2
    chips = pairs * n_head

    vmem = pl.BlockSpec(memory_space=pltpu.VMEM)
    bf16, f32 = jnp.bfloat16, jnp.float32
    dma = pltpu.SemaphoreType.DMA
    wide = jax.ShapeDtypeStruct((tok, heads, per, hd), bf16)
    thin = jax.ShapeDtypeStruct((tok, heads, hd), bf16)
    o, dq, dk, dv = pl.pallas_call(
        functools.partial(kernel, n_seq, n_head, tok),
        out_shape=(wide, wide, thin, thin),
        in_specs=[pl.BlockSpec(memory_space=pltpu.SMEM)] + [vmem] * 4,
        out_specs=(vmem,) * 4,
        scratch_shapes=[
            pltpu.VMEM((heads, 2, GROUP, hd), bf16),
            pltpu.VMEM((heads, 2, GROUP, hd), bf16),
            pltpu.VMEM((heads, 2, HALF, hd), bf16),
            pltpu.VMEM((heads, 2, HALF, hd), bf16),
            pltpu.VMEM((heads, chips, 2, tok, hd), bf16),
            pltpu.VMEM((near, chips, 2, tok, hd), bf16),
            pltpu.VMEM((GROUP, nq), f32),
            pltpu.VMEM((hd, nq), f32),
            pltpu.VMEM((hd, nq), f32),
            pltpu.VMEM((heads, nq, hd), bf16),
            pltpu.VMEM((heads, nq, hd), bf16),
            pltpu.VMEM((heads, 2, tok, hd), f32),
            pltpu.VMEM((heads, tok, hd), bf16),
            pltpu.VMEM((heads, tok, hd), bf16),
            pltpu.SMEM((heads,), jnp.int32),
            pltpu.SMEM((heads,), jnp.int32),
            dma((heads, chips)), dma((heads, chips)), dma((near, chips)), dma((near, chips)),
            dma((heads, pairs)), dma((heads, pairs)), dma((near, pairs)), dma((near, pairs)),
            dma((heads, pairs)), dma((heads, pairs)), dma((near, pairs)), dma((near, pairs)),
            dma((heads, chips)), dma((heads, chips)), dma((near, chips)), dma((near, chips)),
        ],
        compiler_params=pltpu.CompilerParams(
            collective_id=0, has_side_effects=True, vmem_limit_bytes=56 * 1024 * 1024
        ),
    )(shift_amounts, queries, keys, values, d_attended)
    return o, dq, dk, dv


def solution(mesh):
    wide = P(("seq", "head"), None, None, None)
    thin = P(("seq", "head"), None, None)
    return jax.shard_map(
        functools.partial(local, mesh.shape["seq"], mesh.shape["head"]),
        mesh=mesh,
        in_specs=(wide, thin, thin, wide, P()),
        out_specs=(wide, wide, thin, thin),
        check_vma=False,
    )
```

```python
import functools
import math

import jax
import jax.numpy as jnp
from jax import lax
from jax.experimental import pallas as pl
from jax.experimental.pallas import tpu as pltpu
from jax.sharding import PartitionSpec as P

GROUP = 2048
HALF = GROUP // 2
CHUNK = 512
MASKED = -1e30
MESH = pl.DeviceIdType.MESH


def nt(a, b):
    return lax.dot_general(a, b, (((1,), (0,)), ((), ())), preferred_element_type=jnp.float32)


def tn(a, b):
    return lax.dot_general(a, b, (((0,), (0,)), ((), ())), preferred_element_type=jnp.float32)


def kernel(
    n_seq, n_head, tok,
    shift_ref, q_ref, k_ref, v_ref, d_ref,
    o_ref, dq_ref, dk_ref, dv_ref,
    kv, part, sib, red, rb_own, rb_far, scores, o_tr, dq_tr, o_buf, dq_buf, fin, k_by, v_by, q_by, d_by, q_by_tr, d_by_tr, perm, inv,
    own_s, own_r, far_s, far_r, fwd_s, fwd_r, ffwd_s, ffwd_r,
    sib_s, sib_r, fsib_s, fsib_r, back_s, back_r, fback_s, fback_r,
):
    heads = k_ref.shape[1]
    near = heads // 2
    per = q_ref.shape[2]
    nq = per * tok
    span = HALF // (tok * n_head)
    rows = tok * n_head
    pairs = span // 2
    chips = pairs * n_head
    n_planes = n_seq // span
    seq = lax.axis_index("seq")
    x = lax.axis_index("head")
    plane = seq // span
    s_in = seq % span
    y = s_in // 2
    core = s_in % 2
    chip = y * n_head + x
    pos = s_in * n_head + x
    nxt = (plane + 1) % n_planes
    prv = (plane + n_planes - 1) % n_planes
    hd = k_ref.shape[2]
    scaling = 1.0 / math.sqrt(hd)
    to_exp2 = scaling * math.log2(math.e)

    def device(at_plane, at_chip):
        return (at_plane * span + (at_chip // n_head) * 2 + core, at_chip % n_head)

    sibling = (plane * span + y * 2 + 1 - core, x)

    def place(at_chip):
        return ((at_chip // n_head) * 2 + core) * n_head + at_chip % n_head

    barrier = pltpu.get_barrier_semaphore()
    pl.semaphore_signal(barrier, inc=1, device_id=sibling, device_id_type=MESH)
    for k in range(chips):
        other = (chip + k) % chips
        if k:
            pl.semaphore_signal(barrier, inc=1, device_id=device(plane, other), device_id_type=MESH)
        pl.semaphore_signal(barrier, inc=1, device_id=device(nxt, other), device_id_type=MESH)
        pl.semaphore_signal(barrier, inc=1, device_id=device(prv, other), device_id_type=MESH)

    even = plane % 2 == 0
    n_near = jnp.int32(0)
    n_far = jnp.int32(0)
    ranks = []
    for h in range(heads):
        is_near = (shift_ref[h] == 0) == even
        ranks.append(jnp.where(is_near, n_near, (near + n_far) % heads))
        n_near = n_near + is_near.astype(jnp.int32)
        n_far = n_far + 1 - is_near.astype(jnp.int32)
    for h in range(heads):
        inv[h] = ranks[h]
        perm[h] = sum(jnp.where(ranks[j] == h, j, 0) for j in range(heads))

    k_by[...] = jnp.swapaxes(k_ref[...].astype(jnp.float32), 0, 1).astype(jnp.bfloat16)
    v_by[...] = jnp.swapaxes(v_ref[...].astype(jnp.float32), 0, 1).astype(jnp.bfloat16)
    mine = pl.ds(pl.multiple_of(HALF + pos * tok, tok), tok)
    for i in range(heads):
        kv[i, 0, mine, :] = k_by[perm[i]]
        kv[i, 1, mine, :] = v_by[perm[i]]

    def remote(src, dst, ssem, rsem, dev):
        return pltpu.make_async_remote_copy(
            src_ref=src, dst_ref=dst, send_sem=ssem, recv_sem=rsem, device_id=dev, device_id_type=MESH
        )

    def own_copy(i, to):
        view = kv.at[i, :, mine, :]
        return remote(view, view, own_s.at[i, to], own_r.at[i, chip], device(plane, to))

    def own_arrival(i, source):
        view = kv.at[i, :, pl.ds(pl.multiple_of(HALF + place(source) * tok, tok), tok), :]
        return remote(view, view, own_s.at[i, source], own_r.at[i, source], device(plane, source))

    def far_copy(i, to):
        return remote(
            kv.at[i, :, mine, :],
            kv.at[i + near, :, pl.ds(pl.multiple_of(pos * tok, tok), tok), :],
            far_s.at[i, to], far_r.at[i, chip], device(nxt, to),
        )

    def far_arrival(i, source):
        view = kv.at[i, :, pl.ds(pl.multiple_of(place(source) * tok, tok), tok), :]
        return remote(view, view, far_s.at[i - near, source], far_r.at[i - near, source], device(prv, source))

    def strip(base, at_pair, parity):
        return pl.ds(pl.multiple_of(base + (at_pair * 2 + parity) * rows, rows), rows)

    def forward(i, at_pair, parity):
        view = kv.at[i, :, strip(HALF, at_pair, parity), :]
        return remote(view, view, fwd_s.at[i, at_pair], fwd_r.at[i, at_pair], sibling)

    def far_forward(i, at_pair, parity):
        view = kv.at[i, :, strip(0, at_pair, parity), :]
        return remote(view, view, ffwd_s.at[i - near, at_pair], ffwd_r.at[i - near, at_pair], sibling)

    def packed(region, at_pair):
        return pl.ds((region * pairs + at_pair) * rows, rows)

    def sib_copy(i, at_pair):
        return remote(
            part.at[i, :, strip(HALF, at_pair, 1 - core), :], sib.at[i, :, packed(1, at_pair), :],
            sib_s.at[i, at_pair], sib_r.at[i, at_pair], sibling,
        )

    def far_sib_copy(i, at_pair):
        return remote(
            part.at[i, :, strip(0, at_pair, 1 - core), :], sib.at[i, :, packed(0, at_pair), :],
            fsib_s.at[i - near, at_pair], fsib_r.at[i - near, at_pair], sibling,
        )

    def red_rows(region, at_chip):
        return pl.ds(pl.multiple_of(region * (HALF // 2) + at_chip * tok, tok), tok)

    def back_copy(i, to):
        return remote(
            red.at[i, :, red_rows(1, to), :], rb_own.at[i, chip],
            back_s.at[i, to], back_r.at[i, chip], device(plane, to),
        )

    def back_arrival(i, source):
        return remote(
            red.at[i, :, red_rows(1, source), :], rb_own.at[i, source],
            back_s.at[i, source], back_r.at[i, source], device(plane, source),
        )

    def far_back_copy(i, to):
        return remote(
            red.at[i, :, red_rows(0, to), :], rb_far.at[i - near, chip],
            fback_s.at[i - near, to], fback_r.at[i - near, chip], device(prv, to),
        )

    def far_back_arrival(i, source):
        return remote(
            red.at[i, :, red_rows(0, source), :], rb_far.at[i, source],
            fback_s.at[i, source], fback_r.at[i, source], device(nxt, source),
        )

    pl.semaphore_wait(barrier, 3 * chips)

    def order(t):
        return ((t + near - 2) % (heads - 1) + 1) * ((t + heads - 2) // (heads - 1))

    @pl.loop(0, heads)
    def _(t):
        i = order(t)
        for k in range(1, chips):
            to = (chip + k) % chips

            @pl.when(to // n_head >= y)
            def _():
                own_copy(i, to).start()

        @pl.when(i >= near)
        def _():
            for k in range(chips):
                far_copy(i - near, (chip + k) % chips).start()

    def start_forwards(i):
        for k in range(1, chips):
            source = (chip + k) % chips

            @pl.when(source // n_head <= y)
            def _():
                own_arrival(i, source).wait_recv()

        for at_pair in range(pairs):

            @pl.when(at_pair <= y)
            def _():
                forward(i, at_pair, core).start()

        @pl.when(i >= near)
        def _():
            for k in range(chips):
                far_arrival(i, (chip + k) % chips).wait_recv()
            for at_pair in range(pairs):
                far_forward(i, at_pair, core).start()

    def pass_on(i):
        for at_pair in range(pairs):

            @pl.when(at_pair <= y)
            def _():
                sib_copy(i, at_pair).wait_recv()
                for w in range(2):
                    red[i, w, packed(1, at_pair), :] = (
                        part[i, w, strip(HALF, at_pair, core), :].astype(jnp.float32)
                        + sib[i, w, packed(1, at_pair), :].astype(jnp.float32)
                    ).astype(jnp.bfloat16)

        for k in range(1, chips):
            to = (chip + k) % chips

            @pl.when(to // n_head <= y)
            def _():
                back_copy(i, to).start()

        @pl.when(i >= near)
        def _():
            for at_pair in range(pairs):
                far_sib_copy(i, at_pair).wait_recv()
                for w in range(2):
                    red[i, w, packed(0, at_pair), :] = (
                        part[i, w, strip(0, at_pair, core), :].astype(jnp.float32)
                        + sib[i, w, packed(0, at_pair), :].astype(jnp.float32)
                    ).astype(jnp.bfloat16)
            for k in range(chips):
                far_back_copy(i, (chip + k) % chips).start()

    def re_lay(i):
        head = perm[i]
        q = q_ref[:, head].reshape(nq, hd)
        d = d_ref[:, head].reshape(nq, hd)
        q_by[i] = q
        d_by[i] = d
        q_by_tr[i] = q.T
        d_by_tr[i] = d.T

    pl.loop(0, near)(re_lay)
    start_forwards(0)
    pl.loop(near, heads)(re_lay)
    ahead = lax.broadcasted_iota(jnp.int32, (CHUNK, nq), 0) - HALF - pos * tok
    ahead = ahead - lax.broadcasted_iota(jnp.int32, (CHUNK, nq), 1) // per
    n_chunks = (HALF + (y + 1) * 2 * rows) // CHUNK

    @pl.loop(0, heads)
    def _(t):
        i = order(t)
        first = jnp.where(i < near, HALF // CHUNK, 0)
        for at_pair in range(pairs):

            @pl.when(at_pair <= y)
            def _():
                forward(i, at_pair, 1 - core).wait_recv()

        @pl.when(i >= near)
        def _():
            for at_pair in range(pairs):
                far_forward(i, at_pair, 1 - core).wait_recv()

        def score_step(c, top):
            at = pl.ds(pl.multiple_of(c * CHUNK, CHUNK), CHUNK)
            s = nt(kv[i, 0, at, :], q_by_tr[i])
            s = jnp.where(ahead <= -c * CHUNK, s, MASKED)
            scores[at, :] = s
            return jnp.maximum(top, jnp.max(s.reshape(CHUNK // 8, 8, nq), axis=0))

        top = lax.fori_loop(first, n_chunks, score_step, jnp.full((8, nq), MASKED, jnp.float32))
        top = jnp.max(top, axis=0, keepdims=True)
        o_tr[...] = jnp.zeros_like(o_tr)

        @pl.when(t > 0)
        def _():
            pass_on(order(t - 1))

        def prob_step(c, total):
            at = pl.ds(pl.multiple_of(c * CHUNK, CHUNK), CHUNK)
            p = jnp.exp2((scores[at, :] - top) * to_exp2)
            scores[at, :] = p
            o_tr[...] += tn(kv[i, 1, at, :], p.astype(jnp.bfloat16))
            return total + jnp.sum(p.reshape(CHUNK // 8, 8, nq), axis=0)

        total = lax.fori_loop(first, n_chunks, prob_step, jnp.zeros((8, nq), jnp.float32))
        inverse = 1.0 / jnp.sum(total, axis=0, keepdims=True)
        attended = (o_tr[...] * inverse).astype(jnp.bfloat16)
        o_buf[i] = attended.T
        row_dot = jnp.sum(attended.astype(jnp.float32) * d_by_tr[i].astype(jnp.float32), axis=0, keepdims=True)
        dq_tr[...] = jnp.zeros_like(dq_tr)

        @pl.when(t < heads - 1)
        def _():
            start_forwards(order(t + 1))

        @pl.loop(first, n_chunks)
        def _(c):
            at = pl.ds(pl.multiple_of(c * CHUNK, CHUNK), CHUNK)
            k_part = kv[i, 0, at, :]
            p = scores[at, :] * inverse
            ds = (p * (nt(kv[i, 1, at, :], d_by_tr[i]) - row_dot)).astype(jnp.bfloat16)
            part[i, 1, at, :] = nt(p.astype(jnp.bfloat16), d_by[i]).astype(jnp.bfloat16)
            part[i, 0, at, :] = (nt(ds, q_by[i]) * scaling).astype(jnp.bfloat16)
            dq_tr[...] += tn(k_part, ds)

        dq_buf[i] = (dq_tr[...] * scaling).astype(jnp.bfloat16).T
        for at_pair in range(pairs):

            @pl.when(at_pair <= y)
            def _():
                sib_copy(i, at_pair).start()

        @pl.when(i >= near)
        def _():
            for at_pair in range(pairs):
                far_sib_copy(i, at_pair).start()

    pass_on(near - 1)
    for h in range(heads):
        o_ref[:, h] = o_buf[inv[h]].reshape(tok, per, hd)
        dq_ref[:, h] = dq_buf[inv[h]].reshape(tok, per, hd)

    @pl.loop(0, heads)
    def _(i):
        for w in range(2):
            fin[i, w] = red[i, w, red_rows(1, chip), :].astype(jnp.float32)
        for k in range(1, chips):
            source = (chip + k) % chips

            @pl.when(source // n_head >= y)
            def _():
                back_arrival(i, source).wait_recv()
                for w in range(2):
                    fin[i, w] += rb_own[i, source, w].astype(jnp.float32)

        @pl.when(i < near)
        def _():
            for k in range(chips):
                source = (chip + k) % chips
                far_back_arrival(i, source).wait_recv()
                for w in range(2):
                    fin[i, w] += rb_far[i, source, w].astype(jnp.float32)

    dk_ref[...] = jnp.swapaxes(jnp.stack([fin[inv[h], 0] for h in range(heads)]), 0, 1).astype(jnp.bfloat16)
    dv_ref[...] = jnp.swapaxes(jnp.stack([fin[inv[h], 1] for h in range(heads)]), 0, 1).astype(jnp.bfloat16)

    @pl.loop(0, heads)
    def _(i):
        for k in range(1, chips):
            to = (chip + k) % chips

            @pl.when(to // n_head >= y)
            def _():
                own_copy(i, to).wait_send()

            @pl.when(to // n_head <= y)
            def _():
                back_copy(i, to).wait_send()

        for at_pair in range(pairs):

            @pl.when(at_pair <= y)
            def _():
                forward(i, at_pair, core).wait_send()
                sib_copy(i, at_pair).wait_send()

        @pl.when(i < near)
        def _():
            for k in range(chips):
                far_copy(i, (chip + k) % chips).wait_send()

        @pl.when(i >= near)
        def _():
            for k in range(chips):
                far_back_copy(i, (chip + k) % chips).wait_send()
            for at_pair in range(pairs):
                far_forward(i, at_pair, core).wait_send()
                far_sib_copy(i, at_pair).wait_send()


def settle(parts, *refs):
    sems = refs[-1]
    copies = []
    for j in range(4):
        size = refs[j].shape[0] // parts
        for part in range(parts):
            at = pl.ds(part * size, size)
            copies.append(pltpu.make_async_copy(refs[j].at[at], refs[j + 4].at[at], sems.at[j, part]))
    for copy in copies:
        copy.start()
    for copy in copies:
        copy.wait()


def local(n_seq, n_head, queries, keys, values, d_attended, shift_amounts):
    tok, heads, per, hd = queries.shape
    near = heads // 2
    nq = per * tok
    pairs = HALF // (tok * n_head) // 2
    chips = pairs * n_head

    vmem = pl.BlockSpec(memory_space=pltpu.VMEM)
    bf16, f32 = jnp.bfloat16, jnp.float32
    dma = pltpu.SemaphoreType.DMA
    wide = jax.ShapeDtypeStruct((tok, heads, per, hd), bf16)
    thin = jax.ShapeDtypeStruct((tok, heads, hd), bf16)
    results = pl.pallas_call(
        functools.partial(kernel, n_seq, n_head, tok),
        out_shape=(wide, wide, thin, thin),
        in_specs=[pl.BlockSpec(memory_space=pltpu.SMEM)] + [vmem] * 4,
        out_specs=(vmem,) * 4,
        scratch_shapes=[
            pltpu.VMEM((heads, 2, GROUP, hd), bf16),
            pltpu.VMEM((heads, 2, GROUP, hd), bf16),
            pltpu.VMEM((heads, 2, HALF, hd), bf16),
            pltpu.VMEM((heads, 2, HALF, hd), bf16),
            pltpu.VMEM((heads, chips, 2, tok, hd), bf16),
            pltpu.VMEM((near, chips, 2, tok, hd), bf16),
            pltpu.VMEM((GROUP, nq), f32),
            pltpu.VMEM((hd, nq), f32),
            pltpu.VMEM((hd, nq), f32),
            pltpu.VMEM((heads, nq, hd), bf16),
            pltpu.VMEM((heads, nq, hd), bf16),
            pltpu.VMEM((heads, 2, tok, hd), f32),
            pltpu.VMEM((heads, tok, hd), bf16),
            pltpu.VMEM((heads, tok, hd), bf16),
            pltpu.VMEM((heads, nq, hd), bf16),
            pltpu.VMEM((heads, nq, hd), bf16),
            pltpu.VMEM((heads, hd, nq), bf16),
            pltpu.VMEM((heads, hd, nq), bf16),
            pltpu.SMEM((heads,), jnp.int32),
            pltpu.SMEM((heads,), jnp.int32),
            dma((heads, chips)), dma((heads, chips)), dma((near, chips)), dma((near, chips)),
            dma((heads, pairs)), dma((heads, pairs)), dma((near, pairs)), dma((near, pairs)),
            dma((heads, pairs)), dma((heads, pairs)), dma((near, pairs)), dma((near, pairs)),
            dma((heads, chips)), dma((heads, chips)), dma((near, chips)), dma((near, chips)),
        ],
        compiler_params=pltpu.CompilerParams(
            collective_id=0, has_side_effects=True, vmem_limit_bytes=56 * 1024 * 1024
        ),
    )(shift_amounts, queries, keys, values, d_attended)
    parts = 4
    return pl.pallas_call(
        functools.partial(settle, parts),
        out_shape=(wide, wide, thin, thin),
        in_specs=[pl.BlockSpec(memory_space=pl.ANY)] * 4,
        out_specs=(pl.BlockSpec(memory_space=pl.ANY),) * 4,
        scratch_shapes=[dma((4, parts))],
        compiler_params=pltpu.CompilerParams(vmem_limit_bytes=60 * 1024 * 1024),
    )(*results)


def solution(mesh):
    wide = P(("seq", "head"), None, None, None)
    thin = P(("seq", "head"), None, None)
    return jax.shard_map(
        functools.partial(local, mesh.shape["seq"], mesh.shape["head"]),
        mesh=mesh,
        in_specs=(wide, thin, thin, wide, P()),
        out_specs=(wide, wide, thin, thin),
        check_vma=False,
    )
```

```python
import functools
import math

import jax
import jax.numpy as jnp
from jax import lax
from jax.experimental import pallas as pl
from jax.experimental.pallas import tpu as pltpu
from jax.sharding import PartitionSpec as P

GROUP = 2048
HALF = GROUP // 2
MASKED = -1e30
MESH = pl.DeviceIdType.MESH


def nt(a, b):
    return lax.dot_general(a, b, (((1,), (0,)), ((), ())), preferred_element_type=jnp.float32)


def tn(a, b):
    return lax.dot_general(a, b, (((0,), (0,)), ((), ())), preferred_element_type=jnp.float32)


def kernel(
    n_seq, n_head, tok,
    shift_ref, q_ref, k_ref, v_ref, d_ref,
    o_ref, dq_ref, dk_ref, dv_ref,
    kv, part, sib, red, rb_own, rb_far, scores, top8, total8, o_tr, dq_tr, o_buf, dq_buf, fin, k_by, v_by, q_by, d_by, q_by_tr, d_by_tr, perm, inv,
    own_s, own_r, far_s, far_r, fwd_s, fwd_r, ffwd_s, ffwd_r,
    sib_s, sib_r, fsib_s, fsib_r, back_s, back_r, fback_s, fback_r,
):
    heads = k_ref.shape[1]
    near = heads // 2
    per = q_ref.shape[2]
    nq = per * tok
    span = HALF // (tok * n_head)
    rows = tok * n_head
    pairs = span // 2
    chips = pairs * n_head
    n_planes = n_seq // span
    seq = lax.axis_index("seq")
    x = lax.axis_index("head")
    plane = seq // span
    s_in = seq % span
    y = s_in // 2
    core = s_in % 2
    chip = y * n_head + x
    pos = s_in * n_head + x
    nxt = (plane + 1) % n_planes
    prv = (plane + n_planes - 1) % n_planes
    hd = k_ref.shape[2]
    scaling = 1.0 / math.sqrt(hd)
    to_exp2 = scaling * math.log2(math.e)

    def device(at_plane, at_chip):
        return (at_plane * span + (at_chip // n_head) * 2 + core, at_chip % n_head)

    sibling = (plane * span + y * 2 + 1 - core, x)

    def place(at_chip):
        return ((at_chip // n_head) * 2 + core) * n_head + at_chip % n_head

    barrier = pltpu.get_barrier_semaphore()
    pl.semaphore_signal(barrier, inc=1, device_id=sibling, device_id_type=MESH)
    for k in range(chips):
        other = (chip + k) % chips
        if k:
            pl.semaphore_signal(barrier, inc=1, device_id=device(plane, other), device_id_type=MESH)
        pl.semaphore_signal(barrier, inc=1, device_id=device(nxt, other), device_id_type=MESH)
        pl.semaphore_signal(barrier, inc=1, device_id=device(prv, other), device_id_type=MESH)

    even = plane % 2 == 0
    n_near = jnp.int32(0)
    n_far = jnp.int32(0)
    ranks = []
    for h in range(heads):
        is_near = (shift_ref[h] == 0) == even
        ranks.append(jnp.where(is_near, n_near, (near + n_far) % heads))
        n_near = n_near + is_near.astype(jnp.int32)
        n_far = n_far + 1 - is_near.astype(jnp.int32)
    for h in range(heads):
        inv[h] = ranks[h]
        perm[h] = sum(jnp.where(ranks[j] == h, j, 0) for j in range(heads))

    k_by[...] = jnp.swapaxes(k_ref[...].astype(jnp.float32), 0, 1).astype(jnp.bfloat16)
    v_by[...] = jnp.swapaxes(v_ref[...].astype(jnp.float32), 0, 1).astype(jnp.bfloat16)
    mine = pl.ds(pl.multiple_of(HALF + pos * tok, tok), tok)
    for i in range(heads):
        kv[i, 0, mine, :] = k_by[perm[i]]
        kv[i, 1, mine, :] = v_by[perm[i]]

    def remote(src, dst, ssem, rsem, dev):
        return pltpu.make_async_remote_copy(
            src_ref=src, dst_ref=dst, send_sem=ssem, recv_sem=rsem, device_id=dev, device_id_type=MESH
        )

    def own_copy(i, to):
        view = kv.at[i, :, mine, :]
        return remote(view, view, own_s.at[i, to], own_r.at[i, chip], device(plane, to))

    def own_arrival(i, source):
        view = kv.at[i, :, pl.ds(pl.multiple_of(HALF + place(source) * tok, tok), tok), :]
        return remote(view, view, own_s.at[i, source], own_r.at[i, source], device(plane, source))

    def far_copy(i, to):
        return remote(
            kv.at[i, :, mine, :],
            kv.at[i + near, :, pl.ds(pl.multiple_of(pos * tok, tok), tok), :],
            far_s.at[i, to], far_r.at[i, chip], device(nxt, to),
        )

    def far_arrival(i, source):
        view = kv.at[i, :, pl.ds(pl.multiple_of(place(source) * tok, tok), tok), :]
        return remote(view, view, far_s.at[i - near, source], far_r.at[i - near, source], device(prv, source))

    def strip(base, at_pair, parity):
        return pl.ds(pl.multiple_of(base + (at_pair * 2 + parity) * rows, rows), rows)

    def forward(i, at_pair, parity):
        view = kv.at[i, :, strip(HALF, at_pair, parity), :]
        return remote(view, view, fwd_s.at[i, at_pair], fwd_r.at[i, at_pair], sibling)

    def far_forward(i, at_pair, parity):
        view = kv.at[i, :, strip(0, at_pair, parity), :]
        return remote(view, view, ffwd_s.at[i - near, at_pair], ffwd_r.at[i - near, at_pair], sibling)

    def packed(region, at_pair):
        return pl.ds((region * pairs + at_pair) * rows, rows)

    def sib_copy(i, at_pair):
        return remote(
            part.at[i, :, strip(HALF, at_pair, 1 - core), :], sib.at[i, :, packed(1, at_pair), :],
            sib_s.at[i, at_pair], sib_r.at[i, at_pair], sibling,
        )

    def far_sib_copy(i, at_pair):
        return remote(
            part.at[i, :, strip(0, at_pair, 1 - core), :], sib.at[i, :, packed(0, at_pair), :],
            fsib_s.at[i - near, at_pair], fsib_r.at[i - near, at_pair], sibling,
        )

    def red_rows(region, at_chip):
        return pl.ds(pl.multiple_of(region * (HALF // 2) + at_chip * tok, tok), tok)

    def back_copy(i, to):
        return remote(
            red.at[i, :, red_rows(1, to), :], rb_own.at[i, chip],
            back_s.at[i, to], back_r.at[i, chip], device(plane, to),
        )

    def back_arrival(i, source):
        return remote(
            red.at[i, :, red_rows(1, source), :], rb_own.at[i, source],
            back_s.at[i, source], back_r.at[i, source], device(plane, source),
        )

    def far_back_copy(i, to):
        return remote(
            red.at[i, :, red_rows(0, to), :], rb_far.at[i - near, chip],
            fback_s.at[i - near, to], fback_r.at[i - near, chip], device(prv, to),
        )

    def far_back_arrival(i, source):
        return remote(
            red.at[i, :, red_rows(0, source), :], rb_far.at[i, source],
            fback_s.at[i, source], fback_r.at[i, source], device(nxt, source),
        )

    pl.semaphore_wait(barrier, 3 * chips)

    def order(t):
        return ((t + near - 2) % (heads - 1) + 1) * ((t + heads - 2) // (heads - 1))

    @pl.loop(0, heads)
    def _(t):
        i = order(t)
        for k in range(1, chips):
            to = (chip + k) % chips

            @pl.when(to // n_head >= y)
            def _():
                own_copy(i, to).start()

        @pl.when(i >= near)
        def _():
            for k in range(chips):
                far_copy(i - near, (chip + k) % chips).start()

    def start_forwards(i):
        for k in range(1, chips):
            source = (chip + k) % chips

            @pl.when(source // n_head <= y)
            def _():
                own_arrival(i, source).wait_recv()

        for at_pair in range(pairs):

            @pl.when(at_pair <= y)
            def _():
                forward(i, at_pair, core).start()

        @pl.when(i >= near)
        def _():
            for k in range(chips):
                far_arrival(i, (chip + k) % chips).wait_recv()
            for at_pair in range(pairs):
                far_forward(i, at_pair, core).start()

    def pass_on(i):
        for at_pair in range(pairs):

            @pl.when(at_pair <= y)
            def _():
                sib_copy(i, at_pair).wait_recv()
                for w in range(2):
                    red[i, w, packed(1, at_pair), :] = (
                        part[i, w, strip(HALF, at_pair, core), :].astype(jnp.float32)
                        + sib[i, w, packed(1, at_pair), :].astype(jnp.float32)
                    ).astype(jnp.bfloat16)

        for k in range(1, chips):
            to = (chip + k) % chips

            @pl.when(to // n_head <= y)
            def _():
                back_copy(i, to).start()

        @pl.when(i >= near)
        def _():
            for at_pair in range(pairs):
                far_sib_copy(i, at_pair).wait_recv()
                for w in range(2):
                    red[i, w, packed(0, at_pair), :] = (
                        part[i, w, strip(0, at_pair, core), :].astype(jnp.float32)
                        + sib[i, w, packed(0, at_pair), :].astype(jnp.float32)
                    ).astype(jnp.bfloat16)
            for k in range(chips):
                far_back_copy(i, (chip + k) % chips).start()

    def re_lay(i):
        head = perm[i]
        q = q_ref[:, head].reshape(nq, hd)
        d = d_ref[:, head].reshape(nq, hd)
        q_by[i] = q
        d_by[i] = d
        q_by_tr[i] = q.T
        d_by_tr[i] = d.T

    pl.loop(0, near)(re_lay)
    start_forwards(0)
    pl.loop(near, heads)(re_lay)
    short = 2 * rows

    def blocks(i, step):
        @pl.when(i >= near)
        def _():
            step(0, HALF)

        for last in range(pairs):

            @pl.when(y == last)
            def _():
                step(HALF, (last + 1) * short)

    @pl.loop(0, heads)
    def _(t):
        i = order(t)
        for at_pair in range(pairs):

            @pl.when(at_pair <= y)
            def _():
                forward(i, at_pair, 1 - core).wait_recv()

        @pl.when(i >= near)
        def _():
            for at_pair in range(pairs):
                far_forward(i, at_pair, 1 - core).wait_recv()

        top8[...] = jnp.full_like(top8, MASKED)
        total8[...] = jnp.zeros_like(total8)

        def score_step(start, size):
            at = pl.ds(start, size)
            s = nt(kv[i, 0, at, :], q_by_tr[i])
            if start == HALF:
                key_at = lax.broadcasted_iota(jnp.int32, (size, nq), 0)
                query_at = lax.broadcasted_iota(jnp.int32, (1, nq), 1) // per + pos * tok
                s = jnp.where(key_at <= query_at, s, MASKED)
            scores[at, :] = s
            top8[...] = jnp.maximum(top8[...], jnp.max(s.reshape(size // 8, 8, nq), axis=0))

        blocks(i, score_step)
        top = jnp.max(top8[...], axis=0, keepdims=True)
        o_tr[...] = jnp.zeros_like(o_tr)

        @pl.when(t > 0)
        def _():
            pass_on(order(t - 1))

        def prob_step(start, size):
            at = pl.ds(start, size)
            p = jnp.exp2((scores[at, :] - top) * to_exp2)
            scores[at, :] = p
            o_tr[...] += tn(kv[i, 1, at, :], p.astype(jnp.bfloat16))
            total8[...] += jnp.sum(p.reshape(size // 8, 8, nq), axis=0)

        blocks(i, prob_step)
        inverse = 1.0 / jnp.sum(total8[...], axis=0, keepdims=True)
        attended = (o_tr[...] * inverse).astype(jnp.bfloat16)
        o_buf[i] = attended.T
        row_dot = jnp.sum(attended.astype(jnp.float32) * d_by_tr[i].astype(jnp.float32), axis=0, keepdims=True)
        dq_tr[...] = jnp.zeros_like(dq_tr)

        @pl.when(t < heads - 1)
        def _():
            start_forwards(order(t + 1))

        def grad_step(start, size):
            at = pl.ds(start, size)
            k_part = kv[i, 0, at, :]
            p = scores[at, :] * inverse
            ds = (p * (nt(kv[i, 1, at, :], d_by_tr[i]) - row_dot)).astype(jnp.bfloat16)
            part[i, 1, at, :] = nt(p.astype(jnp.bfloat16), d_by[i]).astype(jnp.bfloat16)
            part[i, 0, at, :] = (nt(ds, q_by[i]) * scaling).astype(jnp.bfloat16)
            dq_tr[...] += tn(k_part, ds)

        blocks(i, grad_step)

        dq_buf[i] = (dq_tr[...] * scaling).astype(jnp.bfloat16).T
        for at_pair in range(pairs):

            @pl.when(at_pair <= y)
            def _():
                sib_copy(i, at_pair).start()

        @pl.when(i >= near)
        def _():
            for at_pair in range(pairs):
                far_sib_copy(i, at_pair).start()

    pass_on(near - 1)
    for h in range(heads):
        o_ref[:, h] = o_buf[inv[h]].reshape(tok, per, hd)
        dq_ref[:, h] = dq_buf[inv[h]].reshape(tok, per, hd)

    @pl.loop(0, heads)
    def _(i):
        for w in range(2):
            fin[i, w] = red[i, w, red_rows(1, chip), :].astype(jnp.float32)
        for k in range(1, chips):
            source = (chip + k) % chips

            @pl.when(source // n_head >= y)
            def _():
                back_arrival(i, source).wait_recv()
                for w in range(2):
                    fin[i, w] += rb_own[i, source, w].astype(jnp.float32)

        @pl.when(i < near)
        def _():
            for k in range(chips):
                source = (chip + k) % chips
                far_back_arrival(i, source).wait_recv()
                for w in range(2):
                    fin[i, w] += rb_far[i, source, w].astype(jnp.float32)

    dk_ref[...] = jnp.swapaxes(jnp.stack([fin[inv[h], 0] for h in range(heads)]), 0, 1).astype(jnp.bfloat16)
    dv_ref[...] = jnp.swapaxes(jnp.stack([fin[inv[h], 1] for h in range(heads)]), 0, 1).astype(jnp.bfloat16)

    @pl.loop(0, heads)
    def _(i):
        for k in range(1, chips):
            to = (chip + k) % chips

            @pl.when(to // n_head >= y)
            def _():
                own_copy(i, to).wait_send()

            @pl.when(to // n_head <= y)
            def _():
                back_copy(i, to).wait_send()

        for at_pair in range(pairs):

            @pl.when(at_pair <= y)
            def _():
                forward(i, at_pair, core).wait_send()
                sib_copy(i, at_pair).wait_send()

        @pl.when(i < near)
        def _():
            for k in range(chips):
                far_copy(i, (chip + k) % chips).wait_send()

        @pl.when(i >= near)
        def _():
            for k in range(chips):
                far_back_copy(i, (chip + k) % chips).wait_send()
            for at_pair in range(pairs):
                far_forward(i, at_pair, core).wait_send()
                far_sib_copy(i, at_pair).wait_send()


def settle(parts, *refs):
    sems = refs[-1]
    copies = []
    for j in range(4):
        size = refs[j].shape[0] // parts
        for part in range(parts):
            at = pl.ds(part * size, size)
            copies.append(pltpu.make_async_copy(refs[j].at[at], refs[j + 4].at[at], sems.at[j, part]))
    for copy in copies:
        copy.start()
    for copy in copies:
        copy.wait()


def local(n_seq, n_head, queries, keys, values, d_attended, shift_amounts):
    tok, heads, per, hd = queries.shape
    near = heads // 2
    nq = per * tok
    pairs = HALF // (tok * n_head) // 2
    chips = pairs * n_head

    vmem = pl.BlockSpec(memory_space=pltpu.VMEM)
    bf16, f32 = jnp.bfloat16, jnp.float32
    dma = pltpu.SemaphoreType.DMA
    wide = jax.ShapeDtypeStruct((tok, heads, per, hd), bf16)
    thin = jax.ShapeDtypeStruct((tok, heads, hd), bf16)
    results = pl.pallas_call(
        functools.partial(kernel, n_seq, n_head, tok),
        out_shape=(wide, wide, thin, thin),
        in_specs=[pl.BlockSpec(memory_space=pltpu.SMEM)] + [vmem] * 4,
        out_specs=(vmem,) * 4,
        scratch_shapes=[
            pltpu.VMEM((heads, 2, GROUP, hd), bf16),
            pltpu.VMEM((heads, 2, GROUP, hd), bf16),
            pltpu.VMEM((heads, 2, HALF, hd), bf16),
            pltpu.VMEM((heads, 2, HALF, hd), bf16),
            pltpu.VMEM((heads, chips, 2, tok, hd), bf16),
            pltpu.VMEM((near, chips, 2, tok, hd), bf16),
            pltpu.VMEM((GROUP, nq), f32),
            pltpu.VMEM((8, nq), f32),
            pltpu.VMEM((8, nq), f32),
            pltpu.VMEM((hd, nq), f32),
            pltpu.VMEM((hd, nq), f32),
            pltpu.VMEM((heads, nq, hd), bf16),
            pltpu.VMEM((heads, nq, hd), bf16),
            pltpu.VMEM((heads, 2, tok, hd), f32),
            pltpu.VMEM((heads, tok, hd), bf16),
            pltpu.VMEM((heads, tok, hd), bf16),
            pltpu.VMEM((heads, nq, hd), bf16),
            pltpu.VMEM((heads, nq, hd), bf16),
            pltpu.VMEM((heads, hd, nq), bf16),
            pltpu.VMEM((heads, hd, nq), bf16),
            pltpu.SMEM((heads,), jnp.int32),
            pltpu.SMEM((heads,), jnp.int32),
            dma((heads, chips)), dma((heads, chips)), dma((near, chips)), dma((near, chips)),
            dma((heads, pairs)), dma((heads, pairs)), dma((near, pairs)), dma((near, pairs)),
            dma((heads, pairs)), dma((heads, pairs)), dma((near, pairs)), dma((near, pairs)),
            dma((heads, chips)), dma((heads, chips)), dma((near, chips)), dma((near, chips)),
        ],
        compiler_params=pltpu.CompilerParams(
            collective_id=0, has_side_effects=True, vmem_limit_bytes=56 * 1024 * 1024
        ),
    )(shift_amounts, queries, keys, values, d_attended)
    parts = 4
    return pl.pallas_call(
        functools.partial(settle, parts),
        out_shape=(wide, wide, thin, thin),
        in_specs=[vmem] * 4,
        out_specs=(pl.BlockSpec(memory_space=pl.ANY),) * 4,
        scratch_shapes=[dma((4, parts))],
    )(*results)


def solution(mesh):
    wide = P(("seq", "head"), None, None, None)
    thin = P(("seq", "head"), None, None)
    return jax.shard_map(
        functools.partial(local, mesh.shape["seq"], mesh.shape["head"]),
        mesh=mesh,
        in_specs=(wide, thin, thin, wide, P()),
        out_specs=(wide, wide, thin, thin),
        check_vma=False,
    )
```

```python
import functools
import math

import jax
import jax.numpy as jnp
from jax import lax
from jax.experimental import pallas as pl
from jax.experimental.pallas import tpu as pltpu
from jax.sharding import PartitionSpec as P

GROUP = 2048
HALF = GROUP // 2
MASKED = -1e30
MESH = pl.DeviceIdType.MESH


def nt(a, b):
    return lax.dot_general(a, b, (((1,), (0,)), ((), ())), preferred_element_type=jnp.float32)


def tn(a, b):
    return lax.dot_general(a, b, (((0,), (0,)), ((), ())), preferred_element_type=jnp.float32)


def kernel(
    n_seq, n_head, tok,
    shift_ref, q_ref, k_ref, v_ref, d_ref,
    o_ref, dq_ref, dk_ref, dv_ref,
    kv, part, sib, red, rb_own, rb_far, scores, top8, total8, o_tr, dq_tr, o_buf, dq_buf, fin, k_by, v_by, q_by, d_by, q_by_tr, d_by_tr, perm, inv,
    own_s, own_r, strip_s, strip_r, far_s, far_r, fwd_s, fwd_r, ffwd_s, ffwd_r,
    sib_s, sib_r, fsib_s, fsib_r, back_s, back_r, fback_s, fback_r,
):
    heads = k_ref.shape[1]
    near = heads // 2
    per = q_ref.shape[2]
    nq = per * tok
    span = HALF // (tok * n_head)
    rows = tok * n_head
    pairs = span // 2
    chips = pairs * n_head
    n_planes = n_seq // span
    seq = lax.axis_index("seq")
    x = lax.axis_index("head")
    plane = seq // span
    s_in = seq % span
    y = s_in // 2
    core = s_in % 2
    chip = y * n_head + x
    pos = s_in * n_head + x
    nxt = (plane + 1) % n_planes
    prv = (plane + n_planes - 1) % n_planes
    hd = k_ref.shape[2]
    scaling = 1.0 / math.sqrt(hd)
    to_exp2 = scaling * math.log2(math.e)

    def device(at_plane, at_chip):
        return (at_plane * span + (at_chip // n_head) * 2 + core, at_chip % n_head)

    sibling = (plane * span + y * 2 + 1 - core, x)

    def place(at_chip):
        return ((at_chip // n_head) * 2 + core) * n_head + at_chip % n_head

    barrier = pltpu.get_barrier_semaphore()
    pl.semaphore_signal(barrier, inc=1, device_id=sibling, device_id_type=MESH)
    for k in range(chips):
        other = (chip + k) % chips
        if k:
            pl.semaphore_signal(barrier, inc=1, device_id=device(plane, other), device_id_type=MESH)
        pl.semaphore_signal(barrier, inc=1, device_id=device(nxt, other), device_id_type=MESH)
        pl.semaphore_signal(barrier, inc=1, device_id=device(prv, other), device_id_type=MESH)

    even = plane % 2 == 0
    n_near = jnp.int32(0)
    n_far = jnp.int32(0)
    ranks = []
    for h in range(heads):
        is_near = (shift_ref[h] == 0) == even
        ranks.append(jnp.where(is_near, n_near, (near + n_far) % heads))
        n_near = n_near + is_near.astype(jnp.int32)
        n_far = n_far + 1 - is_near.astype(jnp.int32)
    for h in range(heads):
        inv[h] = ranks[h]
        perm[h] = sum(jnp.where(ranks[j] == h, j, 0) for j in range(heads))

    k_by[...] = jnp.swapaxes(k_ref[...].astype(jnp.float32), 0, 1).astype(jnp.bfloat16)
    v_by[...] = jnp.swapaxes(v_ref[...].astype(jnp.float32), 0, 1).astype(jnp.bfloat16)
    mine = pl.ds(pl.multiple_of(HALF + pos * tok, tok), tok)
    for i in range(heads):
        kv[i, 0, mine, :] = k_by[perm[i]]
        kv[i, 1, mine, :] = v_by[perm[i]]

    def remote(src, dst, ssem, rsem, dev):
        return pltpu.make_async_remote_copy(
            src_ref=src, dst_ref=dst, send_sem=ssem, recv_sem=rsem, device_id=dev, device_id_type=MESH
        )

    def strip(base, at_pair, parity):
        return pl.ds(pl.multiple_of(base + (at_pair * 2 + parity) * rows, rows), rows)

    def own_copy(i, to_x):
        view = kv.at[i, :, mine, :]
        return remote(view, view, own_s.at[i, to_x], own_r.at[i, x], device(plane, y * n_head + to_x))

    def own_arrival(i, from_x):
        view = kv.at[i, :, pl.ds(pl.multiple_of(HALF + place(y * n_head + from_x) * tok, tok), tok), :]
        return remote(view, view, own_s.at[i, from_x], own_r.at[i, from_x], device(plane, y * n_head + from_x))

    def strip_copy(i, to_y):
        view = kv.at[i, :, strip(HALF, y, core), :]
        return remote(view, view, strip_s.at[i, to_y], strip_r.at[i, y], device(plane, to_y * n_head + x))

    def strip_arrival(i, from_y):
        view = kv.at[i, :, strip(HALF, from_y, core), :]
        return remote(view, view, strip_s.at[i, from_y], strip_r.at[i, from_y], device(plane, from_y * n_head + x))

    def far_copy(i, to_y):
        return remote(
            kv.at[i, :, strip(HALF, y, core), :], kv.at[i + near, :, strip(0, y, core), :],
            far_s.at[i, to_y], far_r.at[i, y], device(nxt, to_y * n_head + x),
        )

    def far_arrival(i, from_y):
        view = kv.at[i, :, strip(0, from_y, core), :]
        return remote(
            view, view, far_s.at[i - near, from_y], far_r.at[i - near, from_y], device(prv, from_y * n_head + x)
        )

    def forward(i, at_pair, parity):
        view = kv.at[i, :, strip(HALF, at_pair, parity), :]
        return remote(view, view, fwd_s.at[i, at_pair], fwd_r.at[i, at_pair], sibling)

    def far_forward(i, at_pair, parity):
        view = kv.at[i, :, strip(0, at_pair, parity), :]
        return remote(view, view, ffwd_s.at[i - near, at_pair], ffwd_r.at[i - near, at_pair], sibling)

    def packed(region, at_pair):
        return pl.ds((region * pairs + at_pair) * rows, rows)

    def sib_copy(i, at_pair):
        return remote(
            part.at[i, :, strip(HALF, at_pair, 1 - core), :], sib.at[i, :, packed(1, at_pair), :],
            sib_s.at[i, at_pair], sib_r.at[i, at_pair], sibling,
        )

    def far_sib_copy(i, at_pair):
        return remote(
            part.at[i, :, strip(0, at_pair, 1 - core), :], sib.at[i, :, packed(0, at_pair), :],
            fsib_s.at[i - near, at_pair], fsib_r.at[i - near, at_pair], sibling,
        )

    def red_rows(region, at_chip):
        return pl.ds(pl.multiple_of(region * (HALF // 2) + at_chip * tok, tok), tok)

    def back_copy(i, to):
        return remote(
            red.at[i, :, red_rows(1, to), :], rb_own.at[i, chip],
            back_s.at[i, to], back_r.at[i, chip], device(plane, to),
        )

    def back_arrival(i, source):
        return remote(
            red.at[i, :, red_rows(1, source), :], rb_own.at[i, source],
            back_s.at[i, source], back_r.at[i, source], device(plane, source),
        )

    def far_back_copy(i, to):
        return remote(
            red.at[i, :, red_rows(0, to), :], rb_far.at[i - near, chip],
            fback_s.at[i - near, to], fback_r.at[i - near, chip], device(prv, to),
        )

    def far_back_arrival(i, source):
        return remote(
            red.at[i, :, red_rows(0, source), :], rb_far.at[i, source],
            fback_s.at[i, source], fback_r.at[i, source], device(nxt, source),
        )

    pl.semaphore_wait(barrier, 3 * chips)

    def order(t):
        return ((t + near - 2) % (heads - 1) + 1) * ((t + heads - 2) // (heads - 1))

    @pl.loop(0, heads)
    def _(t):
        i = t // 2 + (t % 2) * near
        for k in range(1, n_head):
            own_copy(i, (x + k) % n_head).start()

    def strip_send(n):
        i = n // 2 + (n % 2) * near
        for k in range(1, n_head):
            own_arrival(i, (x + k) % n_head).wait_recv()
        for to_y in range(1, pairs):

            @pl.when(to_y > y)
            def _():
                strip_copy(i, to_y).start()

        @pl.when(i < near)
        def _():
            for to_y in range(pairs):
                far_copy(i, to_y).start()

    def start_forwards(i):
        for from_y in range(pairs - 1):

            @pl.when(from_y < y)
            def _():
                strip_arrival(i, from_y).wait_recv()

        for at_pair in range(pairs):

            @pl.when(at_pair <= y)
            def _():
                forward(i, at_pair, core).start()

        @pl.when(i >= near)
        def _():
            for from_y in range(pairs):
                far_arrival(i, from_y).wait_recv()
            for at_pair in range(pairs):
                far_forward(i, at_pair, core).start()

    def pass_on(i):
        for at_pair in range(pairs):

            @pl.when(at_pair <= y)
            def _():
                sib_copy(i, at_pair).wait_recv()
                for w in range(2):
                    red[i, w, packed(1, at_pair), :] = (
                        part[i, w, strip(HALF, at_pair, core), :].astype(jnp.float32)
                        + sib[i, w, packed(1, at_pair), :].astype(jnp.float32)
                    ).astype(jnp.bfloat16)

        for k in range(1, chips):
            to = (chip + k) % chips

            @pl.when(to // n_head <= y)
            def _():
                back_copy(i, to).start()

        @pl.when(i >= near)
        def _():
            for at_pair in range(pairs):
                far_sib_copy(i, at_pair).wait_recv()
                for w in range(2):
                    red[i, w, packed(0, at_pair), :] = (
                        part[i, w, strip(0, at_pair, core), :].astype(jnp.float32)
                        + sib[i, w, packed(0, at_pair), :].astype(jnp.float32)
                    ).astype(jnp.bfloat16)
            for k in range(chips):
                far_back_copy(i, (chip + k) % chips).start()

    def re_lay(i):
        head = perm[i]
        q = q_ref[:, head].reshape(nq, hd)
        d = d_ref[:, head].reshape(nq, hd)
        q_by[i] = q
        d_by[i] = d
        q_by_tr[i] = q.T
        d_by_tr[i] = d.T

    @pl.loop(0, 3)
    def _(n):
        pl.loop(n * 2, n * 2 + 2)(re_lay)
        strip_send(n)

    start_forwards(0)
    pl.loop(6, heads)(re_lay)
    short = 2 * rows

    def blocks(i, step):
        @pl.when(i >= near)
        def _():
            step(0, HALF)

        for last in range(pairs):

            @pl.when(y == last)
            def _():
                step(HALF, (last + 1) * short)

    @pl.loop(0, heads)
    def _(t):
        i = order(t)
        for at_pair in range(pairs):

            @pl.when(at_pair <= y)
            def _():
                forward(i, at_pair, 1 - core).wait_recv()

        @pl.when(i >= near)
        def _():
            for at_pair in range(pairs):
                far_forward(i, at_pair, 1 - core).wait_recv()

        top8[...] = jnp.full_like(top8, MASKED)
        total8[...] = jnp.zeros_like(total8)

        def score_step(start, size):
            at = pl.ds(start, size)
            s = nt(kv[i, 0, at, :], q_by_tr[i])
            if start == HALF:
                key_at = lax.broadcasted_iota(jnp.int32, (size, nq), 0)
                query_at = lax.broadcasted_iota(jnp.int32, (1, nq), 1) // per + pos * tok
                s = jnp.where(key_at <= query_at, s, MASKED)
            scores[at, :] = s
            top8[...] = jnp.maximum(top8[...], jnp.max(s.reshape(size // 8, 8, nq), axis=0))

        blocks(i, score_step)
        top = jnp.max(top8[...], axis=0, keepdims=True)
        o_tr[...] = jnp.zeros_like(o_tr)

        @pl.when(t > 0)
        def _():
            pass_on(order(t - 1))

        def prob_step(start, size):
            at = pl.ds(start, size)
            p = jnp.exp2((scores[at, :] - top) * to_exp2)
            scores[at, :] = p
            o_tr[...] += tn(kv[i, 1, at, :], p.astype(jnp.bfloat16))
            total8[...] += jnp.sum(p.reshape(size // 8, 8, nq), axis=0)

        blocks(i, prob_step)
        inverse = 1.0 / jnp.sum(total8[...], axis=0, keepdims=True)
        attended = (o_tr[...] * inverse).astype(jnp.bfloat16)
        o_buf[i] = attended.T
        row_dot = jnp.sum(attended.astype(jnp.float32) * d_by_tr[i].astype(jnp.float32), axis=0, keepdims=True)
        dq_tr[...] = jnp.zeros_like(dq_tr)

        @pl.when(t < 3)
        def _():
            strip_send(3 + 2 * t)

        @pl.when(t < 2)
        def _():
            strip_send(4 + 2 * t)

        @pl.when(t < heads - 1)
        def _():
            start_forwards(order(t + 1))

        def grad_step(start, size):
            at = pl.ds(start, size)
            k_part = kv[i, 0, at, :]
            p = scores[at, :] * inverse
            ds = (p * (nt(kv[i, 1, at, :], d_by_tr[i]) - row_dot)).astype(jnp.bfloat16)
            part[i, 1, at, :] = nt(p.astype(jnp.bfloat16), d_by[i]).astype(jnp.bfloat16)
            part[i, 0, at, :] = (nt(ds, q_by[i]) * scaling).astype(jnp.bfloat16)
            dq_tr[...] += tn(k_part, ds)

        blocks(i, grad_step)

        dq_buf[i] = (dq_tr[...] * scaling).astype(jnp.bfloat16).T
        for at_pair in range(pairs):

            @pl.when(at_pair <= y)
            def _():
                sib_copy(i, at_pair).start()

        @pl.when(i >= near)
        def _():
            for at_pair in range(pairs):
                far_sib_copy(i, at_pair).start()

    pass_on(near - 1)
    for h in range(heads):
        o_ref[:, h] = o_buf[inv[h]].reshape(tok, per, hd)
        dq_ref[:, h] = dq_buf[inv[h]].reshape(tok, per, hd)

    @pl.loop(0, heads)
    def _(i):
        for w in range(2):
            fin[i, w] = red[i, w, red_rows(1, chip), :].astype(jnp.float32)
        for k in range(1, chips):
            source = (chip + k) % chips

            @pl.when(source // n_head >= y)
            def _():
                back_arrival(i, source).wait_recv()
                for w in range(2):
                    fin[i, w] += rb_own[i, source, w].astype(jnp.float32)

        @pl.when(i < near)
        def _():
            for k in range(chips):
                source = (chip + k) % chips
                far_back_arrival(i, source).wait_recv()
                for w in range(2):
                    fin[i, w] += rb_far[i, source, w].astype(jnp.float32)

    dk_ref[...] = jnp.swapaxes(jnp.stack([fin[inv[h], 0] for h in range(heads)]), 0, 1).astype(jnp.bfloat16)
    dv_ref[...] = jnp.swapaxes(jnp.stack([fin[inv[h], 1] for h in range(heads)]), 0, 1).astype(jnp.bfloat16)

    @pl.loop(0, heads)
    def _(i):
        for k in range(1, chips):
            to = (chip + k) % chips

            @pl.when(to // n_head <= y)
            def _():
                back_copy(i, to).wait_send()

        for at_pair in range(pairs):

            @pl.when(at_pair <= y)
            def _():
                forward(i, at_pair, core).wait_send()
                sib_copy(i, at_pair).wait_send()

        for k in range(1, n_head):
            own_copy(i, (x + k) % n_head).wait_send()
        for to_y in range(1, pairs):

            @pl.when(to_y > y)
            def _():
                strip_copy(i, to_y).wait_send()

        @pl.when(i < near)
        def _():
            for to_y in range(pairs):
                far_copy(i, to_y).wait_send()

        @pl.when(i >= near)
        def _():
            for k in range(chips):
                far_back_copy(i, (chip + k) % chips).wait_send()
            for at_pair in range(pairs):
                far_forward(i, at_pair, core).wait_send()
                far_sib_copy(i, at_pair).wait_send()


def settle(parts, *refs):
    sems = refs[-1]
    copies = []
    for j in range(4):
        size = refs[j].shape[0] // parts
        for part in range(parts):
            at = pl.ds(part * size, size)
            copies.append(pltpu.make_async_copy(refs[j].at[at], refs[j + 4].at[at], sems.at[j, part]))
    for copy in copies:
        copy.start()
    for copy in copies:
        copy.wait()


def local(n_seq, n_head, queries, keys, values, d_attended, shift_amounts):
    tok, heads, per, hd = queries.shape
    near = heads // 2
    nq = per * tok
    pairs = HALF // (tok * n_head) // 2
    chips = pairs * n_head

    vmem = pl.BlockSpec(memory_space=pltpu.VMEM)
    bf16, f32 = jnp.bfloat16, jnp.float32
    dma = pltpu.SemaphoreType.DMA
    wide = jax.ShapeDtypeStruct((tok, heads, per, hd), bf16)
    thin = jax.ShapeDtypeStruct((tok, heads, hd), bf16)
    results = pl.pallas_call(
        functools.partial(kernel, n_seq, n_head, tok),
        out_shape=(wide, wide, thin, thin),
        in_specs=[pl.BlockSpec(memory_space=pltpu.SMEM)] + [vmem] * 4,
        out_specs=(vmem,) * 4,
        scratch_shapes=[
            pltpu.VMEM((heads, 2, GROUP, hd), bf16),
            pltpu.VMEM((heads, 2, GROUP, hd), bf16),
            pltpu.VMEM((heads, 2, HALF, hd), bf16),
            pltpu.VMEM((heads, 2, HALF, hd), bf16),
            pltpu.VMEM((heads, chips, 2, tok, hd), bf16),
            pltpu.VMEM((near, chips, 2, tok, hd), bf16),
            pltpu.VMEM((GROUP, nq), f32),
            pltpu.VMEM((8, nq), f32),
            pltpu.VMEM((8, nq), f32),
            pltpu.VMEM((hd, nq), f32),
            pltpu.VMEM((hd, nq), f32),
            pltpu.VMEM((heads, nq, hd), bf16),
            pltpu.VMEM((heads, nq, hd), bf16),
            pltpu.VMEM((heads, 2, tok, hd), f32),
            pltpu.VMEM((heads, tok, hd), bf16),
            pltpu.VMEM((heads, tok, hd), bf16),
            pltpu.VMEM((heads, nq, hd), bf16),
            pltpu.VMEM((heads, nq, hd), bf16),
            pltpu.VMEM((heads, hd, nq), bf16),
            pltpu.VMEM((heads, hd, nq), bf16),
            pltpu.SMEM((heads,), jnp.int32),
            pltpu.SMEM((heads,), jnp.int32),
            dma((heads, n_head)), dma((heads, n_head)), dma((heads, pairs)), dma((heads, pairs)),
            dma((near, pairs)), dma((near, pairs)),
            dma((heads, pairs)), dma((heads, pairs)), dma((near, pairs)), dma((near, pairs)),
            dma((heads, pairs)), dma((heads, pairs)), dma((near, pairs)), dma((near, pairs)),
            dma((heads, chips)), dma((heads, chips)), dma((near, chips)), dma((near, chips)),
        ],
        compiler_params=pltpu.CompilerParams(
            collective_id=0, has_side_effects=True, vmem_limit_bytes=56 * 1024 * 1024
        ),
    )(shift_amounts, queries, keys, values, d_attended)
    parts = 4
    return pl.pallas_call(
        functools.partial(settle, parts),
        out_shape=(wide, wide, thin, thin),
        in_specs=[vmem] * 4,
        out_specs=(pl.BlockSpec(memory_space=pl.ANY),) * 4,
        scratch_shapes=[dma((4, parts))],
    )(*results)


def solution(mesh):
    wide = P(("seq", "head"), None, None, None)
    thin = P(("seq", "head"), None, None)
    return jax.shard_map(
        functools.partial(local, mesh.shape["seq"], mesh.shape["head"]),
        mesh=mesh,
        in_specs=(wide, thin, thin, wide, P()),
        out_specs=(wide, wide, thin, thin),
        check_vma=False,
    )
```

```python
import functools
import math

import jax
import jax.numpy as jnp
from jax import lax
from jax.experimental import pallas as pl
from jax.experimental.pallas import tpu as pltpu
from jax.sharding import PartitionSpec as P

GROUP = 2048
HALF = GROUP // 2
TILE = 256
MASKED = -1e30
MESH = pl.DeviceIdType.MESH


def nt(a, b):
    return lax.dot_general(a, b, (((1,), (0,)), ((), ())), preferred_element_type=jnp.float32)


def tn(a, b):
    return lax.dot_general(a, b, (((0,), (0,)), ((), ())), preferred_element_type=jnp.float32)


def kernel(
    n_seq, n_head, tok,
    shift_ref, q_ref, k_ref, v_ref, d_ref,
    o_ref, dq_ref, dk_ref, dv_ref,
    kv, part, sib, red, rb_own, rb_far, scores, narrow, top8, total8, o_tr, dq_tr, o_buf, dq_buf, fin, k_by, v_by, q_by, d_by, q_by_tr, d_by_tr, perm, inv,
    own_s, own_r, far_s, far_r, fwd_s, fwd_r, ffwd_s, ffwd_r,
    sib_s, sib_r, fsib_s, fsib_r, back_s, back_r, fback_s, fback_r,
):
    heads = k_ref.shape[1]
    near = heads // 2
    per = q_ref.shape[2]
    nq = per * tok
    span = HALF // (tok * n_head)
    rows = tok * n_head
    pairs = span // 2
    chips = pairs * n_head
    n_planes = n_seq // span
    seq = lax.axis_index("seq")
    x = lax.axis_index("head")
    plane = seq // span
    s_in = seq % span
    y = s_in // 2
    core = s_in % 2
    chip = y * n_head + x
    pos = s_in * n_head + x
    nxt = (plane + 1) % n_planes
    prv = (plane + n_planes - 1) % n_planes
    hd = k_ref.shape[2]
    scaling = 1.0 / math.sqrt(hd)
    to_exp2 = scaling * math.log2(math.e)

    def device(at_plane, at_chip):
        return (at_plane * span + (at_chip // n_head) * 2 + core, at_chip % n_head)

    sibling = (plane * span + y * 2 + 1 - core, x)

    def place(at_chip):
        return ((at_chip // n_head) * 2 + core) * n_head + at_chip % n_head

    barrier = pltpu.get_barrier_semaphore()
    pl.semaphore_signal(barrier, inc=1, device_id=sibling, device_id_type=MESH)
    for k in range(chips):
        other = (chip + k) % chips
        if k:
            pl.semaphore_signal(barrier, inc=1, device_id=device(plane, other), device_id_type=MESH)
        pl.semaphore_signal(barrier, inc=1, device_id=device(nxt, other), device_id_type=MESH)
        pl.semaphore_signal(barrier, inc=1, device_id=device(prv, other), device_id_type=MESH)

    even = plane % 2 == 0
    n_near = jnp.int32(0)
    n_far = jnp.int32(0)
    ranks = []
    for h in range(heads):
        is_near = (shift_ref[h] == 0) == even
        ranks.append(jnp.where(is_near, n_near, (near + n_far) % heads))
        n_near = n_near + is_near.astype(jnp.int32)
        n_far = n_far + 1 - is_near.astype(jnp.int32)
    for h in range(heads):
        inv[h] = ranks[h]
        perm[h] = sum(jnp.where(ranks[j] == h, j, 0) for j in range(heads))

    k_by[...] = jnp.swapaxes(k_ref[...].astype(jnp.float32), 0, 1).astype(jnp.bfloat16)
    v_by[...] = jnp.swapaxes(v_ref[...].astype(jnp.float32), 0, 1).astype(jnp.bfloat16)
    mine = pl.ds(pl.multiple_of(HALF + pos * tok, tok), tok)
    for i in range(heads):
        kv[i, 0, mine, :] = k_by[perm[i]]
        kv[i, 1, mine, :] = v_by[perm[i]]

    def remote(src, dst, ssem, rsem, dev):
        return pltpu.make_async_remote_copy(
            src_ref=src, dst_ref=dst, send_sem=ssem, recv_sem=rsem, device_id=dev, device_id_type=MESH
        )

    def own_copy(i, to):
        view = kv.at[i, :, mine, :]
        return remote(view, view, own_s.at[i, to], own_r.at[i, chip], device(plane, to))

    def own_arrival(i, source):
        view = kv.at[i, :, pl.ds(pl.multiple_of(HALF + place(source) * tok, tok), tok), :]
        return remote(view, view, own_s.at[i, source], own_r.at[i, source], device(plane, source))

    def far_copy(i, to):
        return remote(
            kv.at[i, :, mine, :],
            kv.at[i + near, :, pl.ds(pl.multiple_of(pos * tok, tok), tok), :],
            far_s.at[i, to], far_r.at[i, chip], device(nxt, to),
        )

    def far_arrival(i, source):
        view = kv.at[i, :, pl.ds(pl.multiple_of(place(source) * tok, tok), tok), :]
        return remote(view, view, far_s.at[i - near, source], far_r.at[i - near, source], device(prv, source))

    def strip(base, at_pair, parity):
        return pl.ds(pl.multiple_of(base + (at_pair * 2 + parity) * rows, rows), rows)

    def forward(i, at_pair, parity):
        view = kv.at[i, :, strip(HALF, at_pair, parity), :]
        return remote(view, view, fwd_s.at[i, at_pair], fwd_r.at[i, at_pair], sibling)

    def far_forward(i, at_pair, parity):
        view = kv.at[i, :, strip(0, at_pair, parity), :]
        return remote(view, view, ffwd_s.at[i - near, at_pair], ffwd_r.at[i - near, at_pair], sibling)

    def packed(region, at_pair):
        return pl.ds((region * pairs + at_pair) * rows, rows)

    def sib_copy(i, at_pair):
        return remote(
            part.at[i, :, strip(HALF, at_pair, 1 - core), :], sib.at[i, :, packed(1, at_pair), :],
            sib_s.at[i, at_pair], sib_r.at[i, at_pair], sibling,
        )

    def far_sib_copy(i, at_pair):
        return remote(
            part.at[i, :, strip(0, at_pair, 1 - core), :], sib.at[i, :, packed(0, at_pair), :],
            fsib_s.at[i - near, at_pair], fsib_r.at[i - near, at_pair], sibling,
        )

    def red_rows(region, at_chip):
        return pl.ds(pl.multiple_of(region * (HALF // 2) + at_chip * tok, tok), tok)

    def back_copy(i, to):
        return remote(
            red.at[i, :, red_rows(1, to), :], rb_own.at[i, chip],
            back_s.at[i, to], back_r.at[i, chip], device(plane, to),
        )

    def back_arrival(i, source):
        return remote(
            red.at[i, :, red_rows(1, source), :], rb_own.at[i, source],
            back_s.at[i, source], back_r.at[i, source], device(plane, source),
        )

    def far_back_copy(i, to):
        return remote(
            red.at[i, :, red_rows(0, to), :], rb_far.at[i - near, chip],
            fback_s.at[i - near, to], fback_r.at[i - near, chip], device(prv, to),
        )

    def far_back_arrival(i, source):
        return remote(
            red.at[i, :, red_rows(0, source), :], rb_far.at[i, source],
            fback_s.at[i, source], fback_r.at[i, source], device(nxt, source),
        )

    pl.semaphore_wait(barrier, 3 * chips)

    def order(t):
        return ((t + near - 2) % (heads - 1) + 1) * ((t + heads - 2) // (heads - 1))

    @pl.loop(0, heads)
    def _(t):
        i = order(t)
        for k in range(1, chips):
            to = (chip + k) % chips

            @pl.when(to // n_head >= y)
            def _():
                own_copy(i, to).start()

        @pl.when(i >= near)
        def _():
            for k in range(chips):
                far_copy(i - near, (chip + k) % chips).start()

    def start_forwards(i):
        for k in range(1, chips):
            source = (chip + k) % chips

            @pl.when(source // n_head <= y)
            def _():
                own_arrival(i, source).wait_recv()

        for at_pair in range(pairs):

            @pl.when(at_pair <= y)
            def _():
                forward(i, at_pair, core).start()

        @pl.when(i >= near)
        def _():
            for k in range(chips):
                far_arrival(i, (chip + k) % chips).wait_recv()
            for at_pair in range(pairs):
                far_forward(i, at_pair, core).start()

    def pass_on(i):
        for at_pair in range(pairs):

            @pl.when(at_pair <= y)
            def _():
                sib_copy(i, at_pair).wait_recv()
                for w in range(2):
                    red[i, w, packed(1, at_pair), :] = (
                        part[i, w, strip(HALF, at_pair, core), :].astype(jnp.float32)
                        + sib[i, w, packed(1, at_pair), :].astype(jnp.float32)
                    ).astype(jnp.bfloat16)

        for k in range(1, chips):
            to = (chip + k) % chips

            @pl.when(to // n_head <= y)
            def _():
                back_copy(i, to).start()

        @pl.when(i >= near)
        def _():
            for at_pair in range(pairs):
                far_sib_copy(i, at_pair).wait_recv()
                for w in range(2):
                    red[i, w, packed(0, at_pair), :] = (
                        part[i, w, strip(0, at_pair, core), :].astype(jnp.float32)
                        + sib[i, w, packed(0, at_pair), :].astype(jnp.float32)
                    ).astype(jnp.bfloat16)
            for k in range(chips):
                far_back_copy(i, (chip + k) % chips).start()

    def re_lay(i):
        head = perm[i]
        q = q_ref[:, head].reshape(nq, hd)
        d = d_ref[:, head].reshape(nq, hd)
        q_by[i] = q
        d_by[i] = d
        q_by_tr[i] = q.T
        d_by_tr[i] = d.T

    pl.loop(0, near)(re_lay)
    start_forwards(0)
    pl.loop(near, heads)(re_lay)
    short = 2 * rows

    def blocks(i, step):
        @pl.when(i >= near)
        def _():
            step(0, HALF)

        for last in range(pairs):

            @pl.when(y == last)
            def _():
                step(HALF, (last + 1) * short)

    @pl.loop(0, heads)
    def _(t):
        i = order(t)
        for at_pair in range(pairs):

            @pl.when(at_pair <= y)
            def _():
                forward(i, at_pair, 1 - core).wait_recv()

        @pl.when(i >= near)
        def _():
            for at_pair in range(pairs):
                far_forward(i, at_pair, 1 - core).wait_recv()

        top8[...] = jnp.full_like(top8, MASKED)
        total8[...] = jnp.zeros_like(total8)

        def score_step(start, size):
            for r in range(start, start + size, TILE):
                at = pl.ds(r, TILE)
                s = nt(kv[i, 0, at, :], q_by_tr[i])
                if start == HALF:
                    key_at = lax.broadcasted_iota(jnp.int32, (TILE, nq), 0) + (r - HALF)
                    query_at = lax.broadcasted_iota(jnp.int32, (1, nq), 1) // per + pos * tok
                    s = jnp.where(key_at <= query_at, s, MASKED)
                scores[at, :] = s
                top8[...] = jnp.maximum(top8[...], jnp.max(s.reshape(TILE // 8, 8, nq), axis=0))

        blocks(i, score_step)
        top = jnp.max(top8[...], axis=0, keepdims=True)
        o_tr[...] = jnp.zeros_like(o_tr)

        @pl.when(t > 0)
        def _():
            pass_on(order(t - 1))

        def prob_step(start, size):
            for r in range(start, start + size, TILE):
                at = pl.ds(r, TILE)
                p = jnp.exp2((scores[at, :] - top) * to_exp2)
                scores[at, :] = p
                narrow[at, :] = p.astype(jnp.bfloat16)
                total8[...] += jnp.sum(p.reshape(TILE // 8, 8, nq), axis=0)
            at = pl.ds(start, size)
            o_tr[...] += tn(kv[i, 1, at, :], narrow[at, :])

        blocks(i, prob_step)
        inverse = 1.0 / jnp.sum(total8[...], axis=0, keepdims=True)
        attended = (o_tr[...] * inverse).astype(jnp.bfloat16)
        o_buf[i] = attended.T
        row_dot = jnp.sum(attended.astype(jnp.float32) * d_by_tr[i].astype(jnp.float32), axis=0, keepdims=True)
        dq_tr[...] = jnp.zeros_like(dq_tr)

        @pl.when(t < heads - 1)
        def _():
            start_forwards(order(t + 1))

        def grad_step(start, size):
            for r in range(start, start + size, TILE):
                at = pl.ds(r, TILE)
                p = scores[at, :] * inverse
                ds = (p * (nt(kv[i, 1, at, :], d_by_tr[i]) - row_dot)).astype(jnp.bfloat16)
                narrow[at, :] = ds
                part[i, 1, at, :] = nt(p.astype(jnp.bfloat16), d_by[i]).astype(jnp.bfloat16)
                part[i, 0, at, :] = (nt(ds, q_by[i]) * scaling).astype(jnp.bfloat16)
            at = pl.ds(start, size)
            dq_tr[...] += tn(kv[i, 0, at, :], narrow[at, :])

        blocks(i, grad_step)

        dq_buf[i] = (dq_tr[...] * scaling).astype(jnp.bfloat16).T
        for at_pair in range(pairs):

            @pl.when(at_pair <= y)
            def _():
                sib_copy(i, at_pair).start()

        @pl.when(i >= near)
        def _():
            for at_pair in range(pairs):
                far_sib_copy(i, at_pair).start()

    pass_on(near - 1)
    for h in range(heads):
        o_ref[:, h] = o_buf[inv[h]].reshape(tok, per, hd)
        dq_ref[:, h] = dq_buf[inv[h]].reshape(tok, per, hd)

    @pl.loop(0, heads)
    def _(i):
        for w in range(2):
            fin[i, w] = red[i, w, red_rows(1, chip), :].astype(jnp.float32)
        for k in range(1, chips):
            source = (chip + k) % chips

            @pl.when(source // n_head >= y)
            def _():
                back_arrival(i, source).wait_recv()
                for w in range(2):
                    fin[i, w] += rb_own[i, source, w].astype(jnp.float32)

        @pl.when(i < near)
        def _():
            for k in range(chips):
                source = (chip + k) % chips
                far_back_arrival(i, source).wait_recv()
                for w in range(2):
                    fin[i, w] += rb_far[i, source, w].astype(jnp.float32)

    dk_ref[...] = jnp.swapaxes(jnp.stack([fin[inv[h], 0] for h in range(heads)]), 0, 1).astype(jnp.bfloat16)
    dv_ref[...] = jnp.swapaxes(jnp.stack([fin[inv[h], 1] for h in range(heads)]), 0, 1).astype(jnp.bfloat16)

    @pl.loop(0, heads)
    def _(i):
        for k in range(1, chips):
            to = (chip + k) % chips

            @pl.when(to // n_head >= y)
            def _():
                own_copy(i, to).wait_send()

            @pl.when(to // n_head <= y)
            def _():
                back_copy(i, to).wait_send()

        for at_pair in range(pairs):

            @pl.when(at_pair <= y)
            def _():
                forward(i, at_pair, core).wait_send()
                sib_copy(i, at_pair).wait_send()

        @pl.when(i < near)
        def _():
            for k in range(chips):
                far_copy(i, (chip + k) % chips).wait_send()

        @pl.when(i >= near)
        def _():
            for k in range(chips):
                far_back_copy(i, (chip + k) % chips).wait_send()
            for at_pair in range(pairs):
                far_forward(i, at_pair, core).wait_send()
                far_sib_copy(i, at_pair).wait_send()


def settle(parts, *refs):
    sems = refs[-1]
    copies = []
    for j in range(4):
        size = refs[j].shape[0] // parts
        for part in range(parts):
            at = pl.ds(part * size, size)
            copies.append(pltpu.make_async_copy(refs[j].at[at], refs[j + 4].at[at], sems.at[j, part]))
    for copy in copies:
        copy.start()
    for copy in copies:
        copy.wait()


def local(n_seq, n_head, queries, keys, values, d_attended, shift_amounts):
    tok, heads, per, hd = queries.shape
    near = heads // 2
    nq = per * tok
    pairs = HALF // (tok * n_head) // 2
    chips = pairs * n_head

    vmem = pl.BlockSpec(memory_space=pltpu.VMEM)
    bf16, f32 = jnp.bfloat16, jnp.float32
    dma = pltpu.SemaphoreType.DMA
    wide = jax.ShapeDtypeStruct((tok, heads, per, hd), bf16)
    thin = jax.ShapeDtypeStruct((tok, heads, hd), bf16)
    results = pl.pallas_call(
        functools.partial(kernel, n_seq, n_head, tok),
        out_shape=(wide, wide, thin, thin),
        in_specs=[pl.BlockSpec(memory_space=pltpu.SMEM)] + [vmem] * 4,
        out_specs=(vmem,) * 4,
        scratch_shapes=[
            pltpu.VMEM((heads, 2, GROUP, hd), bf16),
            pltpu.VMEM((heads, 2, GROUP, hd), bf16),
            pltpu.VMEM((heads, 2, HALF, hd), bf16),
            pltpu.VMEM((heads, 2, HALF, hd), bf16),
            pltpu.VMEM((heads, chips, 2, tok, hd), bf16),
            pltpu.VMEM((near, chips, 2, tok, hd), bf16),
            pltpu.VMEM((GROUP, nq), f32),
            pltpu.VMEM((GROUP, nq), bf16),
            pltpu.VMEM((8, nq), f32),
            pltpu.VMEM((8, nq), f32),
            pltpu.VMEM((hd, nq), f32),
            pltpu.VMEM((hd, nq), f32),
            pltpu.VMEM((heads, nq, hd), bf16),
            pltpu.VMEM((heads, nq, hd), bf16),
            pltpu.VMEM((heads, 2, tok, hd), f32),
            pltpu.VMEM((heads, tok, hd), bf16),
            pltpu.VMEM((heads, tok, hd), bf16),
            pltpu.VMEM((heads, nq, hd), bf16),
            pltpu.VMEM((heads, nq, hd), bf16),
            pltpu.VMEM((heads, hd, nq), bf16),
            pltpu.VMEM((heads, hd, nq), bf16),
            pltpu.SMEM((heads,), jnp.int32),
            pltpu.SMEM((heads,), jnp.int32),
            dma((heads, chips)), dma((heads, chips)), dma((near, chips)), dma((near, chips)),
            dma((heads, pairs)), dma((heads, pairs)), dma((near, pairs)), dma((near, pairs)),
            dma((heads, pairs)), dma((heads, pairs)), dma((near, pairs)), dma((near, pairs)),
            dma((heads, chips)), dma((heads, chips)), dma((near, chips)), dma((near, chips)),
        ],
        compiler_params=pltpu.CompilerParams(
            collective_id=0, has_side_effects=True, vmem_limit_bytes=56 * 1024 * 1024
        ),
    )(shift_amounts, queries, keys, values, d_attended)
    parts = 4
    return pl.pallas_call(
        functools.partial(settle, parts),
        out_shape=(wide, wide, thin, thin),
        in_specs=[vmem] * 4,
        out_specs=(pl.BlockSpec(memory_space=pl.ANY),) * 4,
        scratch_shapes=[dma((4, parts))],
    )(*results)


def solution(mesh):
    wide = P(("seq", "head"), None, None, None)
    thin = P(("seq", "head"), None, None)
    return jax.shard_map(
        functools.partial(local, mesh.shape["seq"], mesh.shape["head"]),
        mesh=mesh,
        in_specs=(wide, thin, thin, wide, P()),
        out_specs=(wide, wide, thin, thin),
        check_vma=False,
    )
```
